512 devices in a mesh: leaf: 128 (over z, y, core), rhs: 4 (over x).
Axes of the slice: x: 4, y: 4, z: 16, core: 2. Of those that a mesh axis runs over, the one named last changes fastest.
Arguments:
- vectors: bfloat16 [64, 262144], P('rhs', 'leaf'), may hold values from -6 to 6
- near_blocks: bfloat16 [16, 2048, 128, 128], P('rhs', 'leaf'), may hold values from -0.125 to 0.125
- near_src: int32 [16, 2048], P('rhs', 'leaf'), may hold values from 0 to 2047, as said below
- basis: bfloat16 [2048, 64, 128], P('leaf'), may hold values from -0.5 to 0.5
- local_transfer: bfloat16 [1920, 64, 128], P('leaf'), may hold values from -0.625 to 0.625
- leaf_coupling: bfloat16 [2048, 64, 384], P('leaf'), may hold values from -0.3125 to 0.3125
- far_slot: int32 [2048, 6], P('leaf'), may hold values from 0 to 143, as said below
- want_leaf: int32 [128, 128], replicated, may hold values from 0 to 15
- top_transfer: bfloat16 [128, 6, 64, 128], P('leaf'), as said below
- top_coupling: bfloat16 [128, 7, 64, 128], P('leaf'), as said below
Outputs:
- result_vectors: float32 [64, 262144], P('rhs', 'leaf')
The draws below stay inside these ranges and needn't reach their ends.
Inputs may be any that keep to these rules, and one draw needn't show every extreme that they name: near_src[0, t] = t; every entry of column t lies within 16 leaves of t; entries of one column may repeat. `far_slot`: entries below 16 give a leaf of the target's own device by its local index; entry 16 + p stands for the leaf that the target's device requests from device p in want_leaf, where p is never the target's own device; for every leaf the device p of far pair 2 lies 128 / 2 devices away counted round, and those of its other remote pairs lie within 3 devices. top_transfer[d, j - 1] is the transfer matrix of the level-j ancestor of device d's root; all 2**j devices under one ancestor hold equal copies. top_coupling[d, j - 1] holds the two sibling coupling matrices of the level-j ancestor of device d's root; all 2**j devices under one ancestor hold equal copies.
All inputs are finite; a program needn't handle non-finite values.
Results may differ from the reference program's by a relative error of at most 0.029.
Values may be sent and summed in bfloat16 or wider, within the bound.
A program may use at most 128 MiB of HBM per device.

```python
import jax
import jax.numpy as jnp
from jax import lax

LEAF = 128
RANK = 64
VECS = 64
LEAVES_DEV = 16
NEAR = 16
FAR_LOCAL = 2
FAR_REMOTE = 4
FAR = 6
LEAVES = 2048
POINTS = 262144
LOCAL_LEVELS = 4
TOP = 7
TOP_UP = 6
LOCAL_NODES = 1920
N_LEAF = 128


def ancestor_copies(key, levels, scale):
    drawn = jax.random.normal(key, (N_LEAF, levels, RANK, 2 * RANK), jnp.float32) * scale
    device_ids = jnp.arange(N_LEAF, dtype=jnp.int32)
    copies = []
    for height in range(levels):
        leftmost = device_ids >> height + 1 << height + 1
        copies.append(drawn[leftmost, height])
    return jnp.stack(copies, axis=1)


def draw_top_transfer(key, part):
    key = jax.random.fold_in(key, 21)
    return ancestor_copies(key, TOP_UP, (1.5 * RANK) ** (-0.5)).astype(jnp.bfloat16)


def draw_top_coupling(key, part):
    key = jax.random.fold_in(key, 22)
    return ancestor_copies(key, TOP, RANK ** (-0.5)).astype(jnp.bfloat16)


def draw_near_src(key, part):
    key = jax.random.fold_in(key, 11)
    candidates = jnp.concatenate([jnp.arange(-LEAVES_DEV, 0, dtype=jnp.int32), jnp.arange(1, LEAVES_DEV + 1, dtype=jnp.int32)])
    scores = jax.random.randint(key, (LEAVES, 2 * LEAVES_DEV), 0, 1 << 20, dtype=jnp.int32) * (2 * LEAVES_DEV) + jnp.arange(2 * LEAVES_DEV, dtype=jnp.int32)
    ordering = jnp.argsort(scores, axis=1)[:, :NEAR - 1]
    offsets = candidates[ordering]
    target = jnp.arange(LEAVES, dtype=jnp.int32)[:, None]
    shifted = target + offsets
    shifted = jnp.where((shifted < 0) | (shifted >= LEAVES), target - offsets, shifted)
    return jnp.concatenate([target, shifted], axis=1).T.astype(jnp.int32)


def draw_far_slot(key, part):
    key = jax.random.fold_in(key, 12)
    local_key, remote_key = jax.random.split(key)
    spot_count = LEAVES_DEV - 1
    scores = jax.random.randint(local_key, (LEAVES, spot_count), 0, 1 << 20, dtype=jnp.int32) * spot_count + jnp.arange(spot_count, dtype=jnp.int32)
    steps_away = jnp.argsort(scores, axis=1)[:, :FAR_LOCAL].astype(jnp.int32) + 1
    position = jnp.arange(LEAVES, dtype=jnp.int32) % LEAVES_DEV
    local_src = (position[:, None] + steps_away) % LEAVES_DEV
    device_of = jnp.arange(LEAVES, dtype=jnp.int32)[:, None] // LEAVES_DEV
    opposite = (device_of + N_LEAF // 2) % N_LEAF
    device_steps = jnp.concatenate([jnp.arange(-3, 0, dtype=jnp.int32), jnp.arange(1, 4, dtype=jnp.int32)])
    peer_scores = jax.random.randint(remote_key, (LEAVES, 6), 0, 1 << 20, dtype=jnp.int32) * 6 + jnp.arange(6, dtype=jnp.int32)
    peer_pick = jnp.argsort(peer_scores, axis=1)[:, :FAR_REMOTE - 1].astype(jnp.int32)
    peer_steps = device_steps[peer_pick]
    near_dev = device_of + peer_steps
    near_dev = jnp.where((near_dev < 0) | (near_dev >= N_LEAF), device_of - peer_steps, near_dev)
    remote_src = LEAVES_DEV + jnp.concatenate([opposite, near_dev], axis=1)
    return jnp.concatenate([local_src, remote_src], axis=1).astype(jnp.int32)


def set_ends(values, own_key, least, largest):
    spot = [jax.random.randint(jax.random.fold_in(own_key, axis), (), 0, length) for axis, length in enumerate(values.shape)]
    main_axis = values.shape.index(max(values.shape))
    neighbour = spot[:main_axis] + [(spot[main_axis] + 1) % values.shape[main_axis]] + spot[main_axis + 1:]
    return values.at[tuple(spot)].set(least).at[tuple(neighbour)].set(largest)


def shard_levels(own_key, extent, pieces, smallest, largest):
    gain, own = 1.0, jax.random.fold_in(own_key, 6)
    for axis_at, parts in pieces:
        draws = jnp.exp(jax.random.uniform(jax.random.fold_in(own, axis_at), (parts,), jnp.float32, smallest / len(pieces), largest / len(pieces)))
        gain = gain * jnp.repeat(draws, extent[axis_at] // parts).reshape([-1 if axis == axis_at else 1 for axis in range(len(extent))])
    return gain


def noise(stream_key, extent, width, reach, cuts=(), kind=jnp.bfloat16):
    values = jax.random.normal(stream_key, extent, jnp.float32) * width
    if len(cuts) > 0:
        values = shard_levels(stream_key, extent, cuts, -0.22, 0.18) * values
    return jnp.clip(values, min=-reach, max=reach).astype(kind)


def setup_inputs(seed: int = 0) -> dict:
    splits = jax.random.split(jax.random.key(seed), 11)
    return {
        "vectors": noise(splits[0], (VECS, POINTS), 1.0, 6.0, ((0, 4), (1, 128))),
        "near_blocks": noise(splits[1], (NEAR, LEAVES, LEAF, LEAF), (LEAF * NEAR) ** -0.5, 0.125, ((0, 4), (1, 128))),
        "near_src": draw_near_src(jax.random.fold_in(splits[10], 71), 0),
        "basis": noise(splits[3], (LEAVES, RANK, LEAF), LEAF ** -0.5, 0.5, ((0, 128),)),
        "local_transfer": noise(splits[4], (LOCAL_NODES, RANK, 2 * RANK), (3 * RANK // 2) ** -0.5, 0.625, ((0, 128),)),
        "leaf_coupling": noise(splits[5], (LEAVES, RANK, FAR * RANK), (FAR * RANK) ** -0.5, 0.3125, ((0, 128),)),
        "far_slot": draw_far_slot(jax.random.fold_in(splits[10], 71), 0),
        "want_leaf": set_ends(jax.random.randint(splits[7], (N_LEAF, N_LEAF), 0, LEAVES_DEV), jax.random.fold_in(splits[7], 1), 0, LEAVES_DEV - 1).astype(jnp.int32),
        "top_transfer": draw_top_transfer(jax.random.fold_in(splits[10], 71), 0),
        "top_coupling": draw_top_coupling(jax.random.fold_in(splits[10], 71), 0),
    }


def float_product(pattern, lhs_array, rhs_array):
    return jnp.einsum(pattern, lhs_array.astype(jnp.float32), rhs_array.astype(jnp.float32), precision=lax.Precision.HIGHEST)


def level_matrices(local_transfer, height):
    count_now = LEAVES_DEV >> height
    start_at = LEAVES_DEV - (LEAVES_DEV >> (height - 1))
    grouped = local_transfer.reshape(N_LEAF, LEAVES_DEV - 1, RANK, 2 * RANK)
    return grouped[:, start_at:start_at + count_now].reshape(N_LEAF * count_now, RANK, 2 * RANK)


def reference(vectors, near_blocks, near_src, basis, local_transfer, leaf_coupling, far_slot, want_leaf, top_transfer, top_coupling):
    points = vectors.reshape(VECS, LEAVES, LEAF)
    near_part = jnp.zeros((VECS, LEAVES, LEAF), jnp.float32)
    for slot_no in range(NEAR):
        sources = jnp.take(points, near_src[slot_no], axis=1)
        near_part = near_part + float_product('tij,vtj->vti', near_blocks[slot_no], sources)

    up_zero = float_product('tkp,vtp->vtk', basis, points).astype(jnp.bfloat16)
    coeffs = up_zero
    for height in range(1, LOCAL_LEVELS + 1):
        matrices = level_matrices(local_transfer, height)
        paired = coeffs.reshape(VECS, -1, 2 * RANK)
        coeffs = float_product('ckm,vcm->vck', matrices, paired).astype(jnp.bfloat16)

    top_list = [coeffs]
    for height in range(1, TOP):
        count_now = N_LEAF >> height
        owners = jnp.arange(count_now, dtype=jnp.int32) * (1 << height)
        matrices = top_transfer[owners, height - 1]
        paired = top_list[-1].reshape(VECS, count_now, 2 * RANK)
        top_list.append(float_product('ckm,vcm->vck', matrices, paired).astype(jnp.bfloat16))

    down_now = None
    for height in range(TOP, 0, -1):
        count_now = N_LEAF >> height
        owners = jnp.arange(count_now, dtype=jnp.int32) * (1 << height)
        coupling_now = top_coupling[owners, height - 1]
        children = top_list[height - 1].reshape(VECS, count_now, 2, RANK)
        left_down = float_product('ckm,vcm->vck', coupling_now[:, :, :RANK], children[:, :, 1])
        right_down = float_product('ckm,vcm->vck', coupling_now[:, :, RANK:], children[:, :, 0])
        if height < TOP:
            matrices = top_transfer[owners, height - 1]
            spread = float_product('ckm,vck->vcm', matrices, down_now)
            left_down = left_down + spread[:, :, :RANK]
            right_down = right_down + spread[:, :, RANK:]
        down_now = jnp.stack([left_down, right_down], axis=2).reshape(VECS, 2 * count_now, RANK).astype(jnp.bfloat16)

    spread = None
    for height in range(LOCAL_LEVELS, 0, -1):
        matrices = level_matrices(local_transfer, height)
        spread = float_product('ckm,vck->vcm', matrices, down_now).reshape(VECS, -1, RANK)
        if height > 1:
            down_now = spread.astype(jnp.bfloat16)

    owner_dev = jnp.arange(LEAVES, dtype=jnp.int32) // LEAVES_DEV
    peer_dev = jnp.clip(far_slot - LEAVES_DEV, 0, N_LEAF - 1).astype(jnp.int32)
    remote_src = peer_dev * LEAVES_DEV + want_leaf[owner_dev[:, None], peer_dev]
    local_src = owner_dev[:, None] * LEAVES_DEV + far_slot
    src_leaf = jnp.where(far_slot < LEAVES_DEV, local_src, remote_src).astype(jnp.int32)
    gathered = jnp.take(up_zero, src_leaf.reshape(-1), axis=1).reshape(VECS, LEAVES, FAR * RANK)
    coupled = float_product('tkm,vtm->vtk', leaf_coupling, gathered)
    down_zero = (spread + coupled).astype(jnp.bfloat16)
    far_part = float_product('tkp,vtk->vtp', basis, down_zero)
    return (near_part + far_part).reshape(VECS, POINTS)
```

```python
import functools

import jax
import jax.numpy as jnp
from jax import lax
from jax.experimental import pallas as pl
from jax.experimental.pallas import tpu as pltpu
from jax.sharding import PartitionSpec as P

MESH = pl.DeviceIdType.MESH
F32 = jnp.float32
BF16 = jnp.bfloat16
NEAR_CHUNK = 4


def rows_by_rows(lhs, rhs):
    return lax.dot_general(lhs, rhs, (((1,), (1,)), ((), ())), preferred_element_type=F32)


def rows_by_cols(lhs, rhs):
    return lax.dot_general(lhs, rhs, (((1,), (0,)), ((), ())), preferred_element_type=F32)


def twice(matrix):
    return jnp.concatenate([matrix, matrix], axis=0)


def kernel(
    n_leaf,
    n_rhs,
    plane,
    vectors,
    near_blocks,
    near_src,
    basis,
    local_transfer,
    leaf_coupling,
    far_slot,
    want_leaf,
    top_transfer,
    top_coupling,
    out,
    own,
    mine,
    window,
    blocks,
    bases,
    moves,
    couplings,
    top_moves,
    top_couplings,
    src_s,
    far_s,
    want_s,
    leaf_up,
    pool,
    staged,
    message_1,
    arrived_1,
    message_2,
    arrived_2,
    coupled,
    partial,
    others,
    load_sem,
    want_sem,
    gather_send,
    gather_recv,
    side_send,
    side_recv,
    far_send,
    far_recv,
    send_1,
    recv_1,
    send_2,
    recv_2,
    part_send,
    part_recv,
):
    vecs, span = vectors.shape
    leaves, rank, leaf_size = basis.shape
    device = lax.axis_index("leaf")
    row = lax.axis_index("rhs")
    planes = n_leaf // plane
    place = lax.rem(device, plane)
    level = lax.div(device, plane)
    offsets = [1, 2, 3, n_leaf - 1, n_leaf - 2, n_leaf - 3, n_leaf // 2]
    my_rows = pl.ds(pl.multiple_of(row * vecs, vecs), vecs)

    def leaf_at(offset):
        return lax.rem(device + offset, n_leaf)

    def in_plane(where):
        return level * plane + where

    def in_column(where):
        return where * plane + place

    loads = [
        pltpu.make_async_copy(vectors, own, load_sem.at[0]),
        pltpu.make_async_copy(basis, bases, load_sem.at[1]),
        pltpu.make_async_copy(local_transfer, moves, load_sem.at[2]),
        pltpu.make_async_copy(top_transfer.at[0], top_moves, load_sem.at[3]),
        pltpu.make_async_copy(far_slot, far_s, load_sem.at[4]),
        pltpu.make_async_copy(near_src, src_s, load_sem.at[5]),
        pltpu.make_async_copy(near_blocks, blocks, load_sem.at[6]),
        pltpu.make_async_copy(leaf_coupling, couplings, load_sem.at[7]),
        pltpu.make_async_copy(top_coupling.at[0], top_couplings, load_sem.at[8]),
    ]
    wants = [
        pltpu.make_async_copy(
            want_leaf.at[pl.ds(leaf_at(offset), 1)], want_s.at[pl.ds(i, 1)], want_sem.at[i]
        )
        for i, offset in enumerate(offsets)
    ]
    for load in loads + wants:
        load.start()

    barrier = pltpu.get_barrier_semaphore()

    def greet(leaf_index, rhs_index):
        pl.semaphore_signal(
            barrier, inc=1, device_id=(leaf_index, rhs_index), device_id_type=MESH
        )

    for k in range(1, n_rhs):
        greet(device, lax.rem(row + k, n_rhs))
    for offset in offsets:
        greet(leaf_at(offset), row)
    for k in range(1, plane):
        greet(in_plane(lax.rem(place + k, plane)), row)

    def greet_column(k, carry):
        greet(in_column(lax.rem(level + k, planes)), row)
        return carry

    lax.fori_loop(1, planes, greet_column, 0)

    def send(src, dst, send_sem, recv_sem, leaf_index, rhs_index):
        pltpu.make_async_remote_copy(
            src_ref=src,
            dst_ref=dst,
            send_sem=send_sem,
            recv_sem=recv_sem,
            device_id=(leaf_index, rhs_index),
            device_id_type=MESH,
        ).start()

    def wait_bytes(ref, sem):
        pltpu.make_async_copy(ref, ref, sem).wait()

    loads[0].wait()
    points = [own[:, t * leaf_size : (t + 1) * leaf_size] for t in range(leaves)]
    for t in range(leaves):
        mine[t] = points[t]
        window[leaves + t, my_rows] = points[t]
    pl.semaphore_wait(barrier, (n_rhs - 1) + len(offsets) + (plane - 1) + (planes - 1))

    before, centre, after = (pl.ds(i * leaves, leaves) for i in range(3))
    for k in range(1, n_rhs):
        send(
            mine,
            window.at[centre, my_rows],
            gather_send,
            gather_recv.at[k - 1],
            device,
            lax.rem(row + k, n_rhs),
        )
    send(mine, window.at[before, my_rows], side_send.at[0], side_recv.at[0], leaf_at(1), row)
    send(
        mine, window.at[after, my_rows], side_send.at[1], side_recv.at[1], leaf_at(n_leaf - 1), row
    )

    lanes = lax.broadcasted_iota(jnp.int32, (vecs, 2 * rank), 1)
    low = lanes < rank

    def in_half(value, side):
        return jnp.where((lanes >= rank) == (side == 1), value, 0.0).astype(BF16)

    def both(product):
        return jnp.where(low, product[:vecs], product[vecs:])

    def pair_of(ref, node):
        return ref[node : node + 2].reshape(2 * rank, -1)

    loads[1].wait()
    pairs = []
    for c in range(leaves // 2):
        rows = jnp.concatenate([points[2 * c], points[2 * c + 1]], axis=0)
        pair = both(rows_by_rows(rows, pair_of(bases, 2 * c)))
        turned = pltpu.roll(pair, rank, 1)
        for leaf, value in (
            (2 * c, jnp.where(low, pair, turned).astype(BF16)),
            (2 * c + 1, jnp.where(low, turned, pair).astype(BF16)),
        ):
            leaf_up[leaf] = value
            pool[leaf] = value
        pairs.append(pair.astype(BF16))
    loads[2].wait()
    start = 0
    while len(pairs) > 1:
        nodes = len(pairs)
        pairs = [
            both(
                rows_by_rows(
                    jnp.concatenate([pairs[c], pairs[c + 1]], axis=0), pair_of(moves, start + c)
                )
            ).astype(BF16)
            for c in range(0, nodes, 2)
        ]
        start += nodes
    root = rows_by_rows(pairs[0], twice(moves[start]))

    loads[3].wait()
    plane_levels = plane.bit_length() - 1
    column_levels = planes.bit_length() - 1
    top_levels = plane_levels + column_levels

    def side_at(height):
        return lax.rem(lax.div(device, 1 << height - 1), 2)

    def lifted(value, height):
        return rows_by_rows(in_half(value, side_at(height)), twice(top_moves[height - 1]))

    def sibling_start(position, height):
        width = 1 << height - 1
        block = lax.div(position, width)
        return (block + 1 - 2 * lax.rem(block, 2)) * width

    shares = [root]
    for height in range(1, plane_levels + 1):
        shares.append(lifted(shares[-1], height))
    whole_share = shares[plane_levels].astype(BF16)
    for height in range(1, plane_levels + 1):
        message_1[height - 1] = jnp.concatenate(
            [shares[height - 1].astype(BF16), whole_share], axis=1
        )
    arrived_1[place] = message_1[0]
    for height in range(1, plane_levels + 1):
        for i in range(1 << height - 1):
            send(
                message_1.at[height - 1],
                arrived_1.at[place],
                send_1,
                recv_1,
                in_plane(sibling_start(place, height) + i),
                row,
            )

    for i, offset in enumerate(offsets):
        wants[i].wait()
        staged[i] = leaf_up[want_s[i, device]]
        send(
            staged.at[i], pool.at[leaves + device], far_send, far_recv, leaf_at(offset), row
        )

    for k in range(1, n_rhs):
        theirs = pl.ds(pl.multiple_of(lax.rem(row + n_rhs - k, n_rhs) * vecs, vecs), vecs)
        piece = window.at[centre, theirs]
        wait_bytes(piece, gather_recv.at[k - 1])
        send(piece, window.at[before, theirs], side_send.at[0], side_recv.at[0], leaf_at(1), row)
        send(
            piece,
            window.at[after, theirs],
            side_send.at[1],
            side_recv.at[1],
            leaf_at(n_leaf - 1),
            row,
        )

    wait_bytes(arrived_1.at[pl.ds(0, plane - 1)], recv_1)
    siblings = []
    for height in range(1, plane_levels + 1):
        first = sibling_start(place, height)
        siblings.append(
            sum(arrived_1[first + i].astype(F32)[:, : 2 * rank] for i in range(1 << height - 1))
        )
    plane_up = sum(arrived_1[i].astype(F32)[:, 2 * rank :] for i in range(plane))
    share = plane_up
    for height in range(plane_levels + 1, top_levels + 1):
        if height > plane_levels + 1:
            share = lifted(share, height - 1)
        message_2[height - plane_levels - 1] = share.astype(BF16)
    for height in range(1, column_levels + 1):
        first = sibling_start(level, height)

        def send_column(i, carry, height=height, first=first):
            send(
                message_2.at[height - 1],
                arrived_2.at[level],
                send_2,
                recv_2,
                in_column(first + i),
                row,
            )
            return carry

        lax.fori_loop(0, 1 << height - 1, send_column, 0)

    wait_bytes(staged, far_recv)
    loads[4].wait()
    loads[7].wait()

    def far_block(leaf, f):
        return pool[far_s[f, leaf]].astype(F32)

    far = couplings.shape[2] // rank

    def far_row(leaf):
        return jnp.concatenate(
            [
                jnp.where(low, far_block(leaf, f), far_block(leaf, f + 1)).astype(BF16)
                for f in range(0, far, 2)
            ],
            axis=1,
        )

    for c in range(leaves // 2):
        sources = jnp.concatenate([far_row(2 * c), far_row(2 * c + 1)], axis=0)
        coupled[c] = both(rows_by_rows(sources, pair_of(couplings, 2 * c)))

    loads[5].wait()
    loads[6].wait()
    wait_bytes(window.at[before], side_recv.at[0])
    wait_bytes(window.at[after], side_recv.at[1])
    slots = blocks.shape[0]
    first_leaf = (device - 1) * leaves
    width = NEAR_CHUNK * leaf_size
    for chunk in range(leaves // NEAR_CHUNK):
        for leaf in range(chunk * NEAR_CHUNK, (chunk + 1) * NEAR_CHUNK):
            sources = jnp.concatenate(
                [
                    window[(src_s[q, leaf] - first_leaf) & (window.shape[0] - 1)] for q in range(slots)
                ],
                axis=1,
            )
            matrix = jnp.concatenate([blocks[q, leaf] for q in range(slots)], axis=1)
            partial[:, leaf * leaf_size : (leaf + 1) * leaf_size] = rows_by_rows(
                sources, matrix
            ).astype(BF16)
        cols = pl.ds(chunk * width, width)
        for k in range(1, n_rhs):
            target = lax.rem(row + k, n_rhs)
            theirs = pl.ds(pl.multiple_of(target * vecs, vecs), vecs)
            send(
                partial.at[theirs, cols],
                others.at[k - 1, :, cols],
                part_send,
                part_recv,
                device,
                target,
            )

    wait_bytes(arrived_2.at[pl.ds(0, planes - 1)], recv_2)
    for height in range(1, column_levels + 1):
        first = sibling_start(level, height)
        siblings.append(sum(arrived_2[first + i].astype(F32) for i in range(1 << height - 1)))
    loads[8].wait()
    terms = [
        rows_by_rows(in_half(siblings[height - 1], side_at(height)), twice(top_couplings[height - 1]))
        for height in range(1, top_levels + 1)
    ]
    down = in_half(terms[top_levels - 1], side_at(top_levels))
    for height in range(top_levels - 1, 0, -1):
        spread = rows_by_cols(down, twice(top_moves[height - 1]))
        down = in_half(terms[height - 1] + spread, side_at(height))

    def split(pair):
        return jnp.concatenate(
            [jnp.where(low, pair, 0.0), jnp.where(low, 0.0, pair)], axis=0
        ).astype(BF16)

    pairs = [rows_by_cols(down, twice(moves[start]))]
    while len(pairs) < leaves // 2:
        start -= 2 * len(pairs)
        spreads = [
            rows_by_cols(split(pair), pair_of(moves, start + 2 * c))
            for c, pair in enumerate(pairs)
        ]
        pairs = [half for both_now in spreads for half in (both_now[:vecs], both_now[vecs:])]

    wait_bytes(others, part_recv)
    for c, pair in enumerate(pairs):
        far_part = rows_by_cols(split(pair + coupled[c]), pair_of(bases, 2 * c))
        for leaf, value in ((2 * c, far_part[:vecs]), (2 * c + 1, far_part[vecs:])):
            cols = slice(leaf * leaf_size, (leaf + 1) * leaf_size)
            total = value + partial[my_rows, cols].astype(F32)
            for k in range(n_rhs - 1):
                total = total + others[k, :, cols].astype(F32)
            out[:, cols] = total

    if n_rhs > 1:
        wait_bytes(others, gather_send)
        wait_bytes(others, part_send)
    wait_bytes(window.at[before], side_send.at[0])
    wait_bytes(window.at[after], side_send.at[1])
    wait_bytes(staged, far_send)
    wait_bytes(arrived_1.at[pl.ds(0, plane - 1)], send_1)
    wait_bytes(arrived_2.at[pl.ds(0, planes - 1)], send_2)


def local(n_leaf, n_rhs, plane, *arrays):
    (vectors, near_blocks, near_src, basis, local_transfer, leaf_coupling, far_slot) = arrays[:7]
    want_leaf, top_transfer, top_coupling = arrays[7:]
    vecs, span = vectors.shape
    leaves, rank, leaf_size = basis.shape
    far_slot = far_slot.T
    planes = n_leaf // plane
    levels = plane.bit_length() - 1, planes.bit_length() - 1
    dma = pltpu.SemaphoreType.DMA
    scratch = [
        pltpu.VMEM((vecs, span), BF16),
        pltpu.VMEM((leaves, vecs, leaf_size), BF16),
        pltpu.VMEM((4 * leaves, n_rhs * vecs, leaf_size), BF16),
        pltpu.VMEM(near_blocks.shape, BF16),
        pltpu.VMEM(basis.shape, BF16),
        pltpu.VMEM(local_transfer.shape, BF16),
        pltpu.VMEM(leaf_coupling.shape, BF16),
        pltpu.VMEM(top_transfer.shape[1:], BF16),
        pltpu.VMEM(top_coupling.shape[1:], BF16),
        pltpu.SMEM(near_src.shape, jnp.int32),
        pltpu.SMEM(far_slot.shape, jnp.int32),
        pltpu.SMEM((7, n_leaf), jnp.int32),
        pltpu.VMEM((leaves, vecs, 2 * rank), BF16),
        pltpu.VMEM((leaves + n_leaf, vecs, 2 * rank), BF16),
        pltpu.VMEM((7, vecs, 2 * rank), BF16),
        pltpu.VMEM((levels[0], vecs, 4 * rank), BF16),
        pltpu.VMEM((plane, vecs, 4 * rank), BF16),
        pltpu.VMEM((levels[1], vecs, 2 * rank), BF16),
        pltpu.VMEM((planes, vecs, 2 * rank), BF16),
        pltpu.VMEM((leaves // 2, vecs, 2 * rank), F32),
        pltpu.VMEM((n_rhs * vecs, span), BF16),
        pltpu.VMEM((max(n_rhs - 1, 1), vecs, span), BF16),
        dma((9,)),
        dma((7,)),
        dma,
        dma((max(n_rhs - 1, 1),)),
        dma((2,)),
        dma((2,)),
        dma,
        dma,
        dma,
        dma,
        dma,
        dma,
        dma,
        dma,
    ]
    return pl.pallas_call(
        functools.partial(kernel, n_leaf, n_rhs, plane),
        out_shape=jax.ShapeDtypeStruct((vecs, span), F32),
        in_specs=[pl.BlockSpec(memory_space=pltpu.HBM)] * 10,
        out_specs=pl.BlockSpec(memory_space=pltpu.VMEM),
        scratch_shapes=scratch,
        compiler_params=pltpu.CompilerParams(
            collective_id=0, has_side_effects=True, vmem_limit_bytes=60 << 20
        ),
        name="hierarchical_product",
    )(
        vectors,
        near_blocks,
        near_src,
        basis,
        local_transfer,
        leaf_coupling,
        far_slot,
        want_leaf,
        top_transfer,
        top_coupling,
    )


def solution(mesh):
    in_specs = (
        P("rhs", "leaf"),
        P("rhs", "leaf", None, None),
        P("rhs", "leaf"),
        P("leaf", None, None),
        P("leaf", None, None),
        P("leaf", None, None),
        P("leaf", None),
        P(),
        P("leaf", None, None, None),
        P("leaf", None, None, None),
    )
    body = functools.partial(local, mesh.shape["leaf"], mesh.shape["rhs"], 8)
    return jax.shard_map(
        body, mesh=mesh, in_specs=in_specs, out_specs=P("rhs", "leaf"), check_vma=False
    )
```

```python
import functools

import jax
import jax.numpy as jnp
from jax import lax
from jax.experimental import pallas as pl
from jax.experimental.pallas import tpu as pltpu
from jax.sharding import PartitionSpec as P

MESH = pl.DeviceIdType.MESH
F32 = jnp.float32
BF16 = jnp.bfloat16
NEAR_CHUNK = 4


def rows_by_rows(lhs, rhs):
    return lax.dot_general(lhs, rhs, (((1,), (1,)), ((), ())), preferred_element_type=F32)


def rows_by_cols(lhs, rhs):
    return lax.dot_general(lhs, rhs, (((1,), (0,)), ((), ())), preferred_element_type=F32)


def twice(matrix):
    return jnp.concatenate([matrix, matrix], axis=0)


def kernel(
    n_leaf,
    n_rhs,
    plane,
    vectors,
    near_blocks,
    near_src,
    basis,
    local_transfer,
    leaf_coupling,
    far_slot,
    want_leaf,
    top_transfer,
    top_coupling,
    out,
    own,
    mine,
    window,
    blocks,
    bases,
    moves,
    couplings,
    top_moves,
    top_couplings,
    src_s,
    far_s,
    want_s,
    leaf_up,
    pool,
    staged,
    message_1,
    arrived_1,
    message_2,
    arrived_2,
    coupled,
    partial,
    others,
    load_sem,
    want_sem,
    gather_send,
    gather_recv,
    side_send,
    side_recv,
    far_send,
    far_recv,
    send_1,
    recv_1,
    send_2,
    recv_2,
    part_send,
    part_recv,
    ready,
):
    vecs, span = vectors.shape
    leaves, rank, leaf_size = basis.shape
    device = lax.axis_index("leaf")
    row = lax.axis_index("rhs")
    planes = n_leaf // plane
    place = lax.rem(device, plane)
    level = lax.div(device, plane)
    offsets = [1, 2, 3, n_leaf - 1, n_leaf - 2, n_leaf - 3, n_leaf // 2]
    my_rows = pl.ds(pl.multiple_of(row * vecs, vecs), vecs)

    def leaf_at(offset):
        return lax.rem(device + offset, n_leaf)

    def in_plane(where):
        return level * plane + where

    def in_column(where):
        return where * plane + place

    loads = [
        pltpu.make_async_copy(vectors, own, load_sem.at[0]),
        pltpu.make_async_copy(basis, bases, load_sem.at[1]),
        pltpu.make_async_copy(local_transfer, moves, load_sem.at[2]),
        pltpu.make_async_copy(top_transfer.at[0], top_moves, load_sem.at[3]),
        pltpu.make_async_copy(far_slot, far_s, load_sem.at[4]),
        pltpu.make_async_copy(near_src, src_s, load_sem.at[5]),
        pltpu.make_async_copy(near_blocks, blocks, load_sem.at[6]),
        pltpu.make_async_copy(leaf_coupling, couplings, load_sem.at[7]),
        pltpu.make_async_copy(top_coupling.at[0], top_couplings, load_sem.at[8]),
    ]
    wants = [
        pltpu.make_async_copy(
            want_leaf.at[pl.ds(leaf_at(offset), 1)], want_s.at[pl.ds(i, 1)], want_sem.at[i]
        )
        for i, offset in enumerate(offsets)
    ]
    for load in loads + wants:
        load.start()

    barrier = pltpu.get_barrier_semaphore()

    def greet(leaf_index, rhs_index):
        pl.semaphore_signal(
            barrier, inc=1, device_id=(leaf_index, rhs_index), device_id_type=MESH
        )

    def loop(first, last, step):
        def body(i, carry):
            step(i)
            return carry

        lax.fori_loop(first, last, body, 0)

    steps = range(1, 4)
    for k in range(1, n_rhs):
        greet(device, lax.rem(row + k, n_rhs))
    for k in range(1, plane):
        greet(in_plane(lax.rem(place + k, plane)), row)
    for k in steps:
        greet(leaf_at(n_leaf - k), row)
        pl.when(device + k < n_leaf)(functools.partial(greet, leaf_at(k), row))
    loop(level + 1, planes, lambda other: greet(in_column(other), row))
    behind = sum((device >= k).astype(jnp.int32) for k in steps)
    greetings = (n_rhs - 1) + (plane - 1) + len(steps) + behind + level

    def send(src, dst, send_sem, recv_sem, leaf_index, rhs_index):
        pltpu.make_async_remote_copy(
            src_ref=src,
            dst_ref=dst,
            send_sem=send_sem,
            recv_sem=recv_sem,
            device_id=(leaf_index, rhs_index),
            device_id_type=MESH,
        ).start()

    def wait_bytes(ref, sem):
        pltpu.make_async_copy(ref, ref, sem).wait()

    lanes = lax.broadcasted_iota(jnp.int32, (vecs, 2 * rank), 1)
    low = lanes < rank

    def in_half(value, side):
        return jnp.where((lanes >= rank) == (side == 1), value, 0.0).astype(BF16)

    def both(product):
        return jnp.where(low, product[:vecs], product[vecs:])

    def pair_of(ref, node):
        return ref[node : node + 2].reshape(2 * rank, -1)

    loads[0].wait()
    points = [own[:, t * leaf_size : (t + 1) * leaf_size] for t in range(leaves)]
    loads[1].wait()
    ups = []
    for c in range(leaves // 2):
        rows = jnp.concatenate([points[2 * c], points[2 * c + 1]], axis=0)
        ups.append(both(rows_by_rows(rows, pair_of(bases, 2 * c))))
    pairs = [pair.astype(BF16) for pair in ups]
    loads[2].wait()
    start = 0
    while len(pairs) > 1:
        nodes = len(pairs)
        pairs = [
            both(
                rows_by_rows(
                    jnp.concatenate([pairs[c], pairs[c + 1]], axis=0), pair_of(moves, start + c)
                )
            ).astype(BF16)
            for c in range(0, nodes, 2)
        ]
        start += nodes
    root = rows_by_rows(pairs[0], twice(moves[start]))

    loads[3].wait()
    plane_levels = plane.bit_length() - 1
    column_levels = planes.bit_length() - 1
    top_levels = plane_levels + column_levels

    def side_at(height):
        return lax.rem(lax.div(device, 1 << height - 1), 2)

    def lifted(value, height):
        return rows_by_rows(in_half(value, side_at(height)), twice(top_moves[height - 1]))

    def sibling_start(position, height):
        width = 1 << height - 1
        block = lax.div(position, width)
        return (block + 1 - 2 * lax.rem(block, 2)) * width

    shares = [root]
    for height in range(1, plane_levels + 1):
        shares.append(lifted(shares[-1], height))
    whole_share = shares[plane_levels].astype(BF16)
    for height in range(1, plane_levels + 1):
        message_1[height - 1] = jnp.concatenate(
            [shares[height - 1].astype(BF16), whole_share], axis=1
        )
    arrived_1[place] = message_1[0]

    pl.semaphore_wait(barrier, greetings)
    for height in range(plane_levels, 0, -1):
        for i in range(1 << height - 1):
            send(
                message_1.at[height - 1],
                arrived_1.at[place],
                send_1,
                recv_1,
                in_plane(sibling_start(place, height) + i),
                row,
            )

    def tell(other):
        pl.semaphore_signal(
            ready, inc=1, device_id=(in_column(other), row), device_id_type=MESH
        )

    loop(0, level, tell)
    for k in steps:

        @pl.when(device + k >= n_leaf)
        def _(k=k):
            pl.semaphore_signal(
                ready, inc=1, device_id=(leaf_at(k), row), device_id_type=MESH
            )

    for t in range(leaves):
        mine[t] = points[t]
        window[leaves + t, my_rows] = points[t]
    before, centre, after = (pl.ds(i * leaves, leaves) for i in range(3))
    for k in (2, 1, 3):
        if k < n_rhs:
            send(
                mine,
                window.at[centre, my_rows],
                gather_send,
                gather_recv.at[k - 1],
                device,
                lax.rem(row + k, n_rhs),
            )

    def to_neighbours(piece, rows):
        @pl.when(device + 1 < n_leaf)
        def _():
            send(
                piece, window.at[before, rows], side_send.at[0], side_recv.at[0], leaf_at(1), row
            )

        @pl.when(device > 0)
        def _():
            send(
                piece,
                window.at[after, rows],
                side_send.at[1],
                side_recv.at[1],
                leaf_at(n_leaf - 1),
                row,
            )

    to_neighbours(mine, my_rows)

    for c, pair in enumerate(ups):
        turned = pltpu.roll(pair, rank, 1)
        for leaf, value in (
            (2 * c, jnp.where(low, pair, turned).astype(BF16)),
            (2 * c + 1, jnp.where(low, turned, pair).astype(BF16)),
        ):
            leaf_up[leaf] = value
            pool[leaf] = value

    def send_far(i):
        send(
            staged.at[i],
            pool.at[leaves + device],
            far_send,
            far_recv,
            leaf_at(offsets[i]),
            row,
        )

    def far_goes_early(i):
        offset = offsets[i]
        if offset <= 3:
            return None
        return device >= n_leaf - offset

    for i, offset in enumerate(offsets):
        wants[i].wait()
        staged[i] = leaf_up[want_s[i, device]]
        early = far_goes_early(i)
        if early is None:
            send_far(i)
        else:
            pl.when(early)(functools.partial(send_far, i))

    wait_bytes(arrived_1.at[pl.ds(0, plane - 1)], recv_1)
    plane_up = sum(arrived_1[i].astype(F32)[:, 2 * rank :] for i in range(plane))
    share = plane_up
    for height in range(plane_levels + 1, top_levels + 1):
        if height > plane_levels + 1:
            share = lifted(share, height - 1)
        message_2[height - plane_levels - 1] = share.astype(BF16)

    def send_column(height):
        first = sibling_start(level, height)

        def one(i):
            send(
                message_2.at[height - 1],
                arrived_2.at[level],
                send_2,
                recv_2,
                in_column(first + i),
                row,
            )

        loop(0, 1 << height - 1, one)

    for height in range(column_levels, 0, -1):
        pl.when(side_at(plane_levels + height) == 1)(functools.partial(send_column, height))

    for k in (1, 3, 2):
        if k < n_rhs:
            theirs = pl.ds(pl.multiple_of(lax.rem(row + n_rhs - k, n_rhs) * vecs, vecs), vecs)
            piece = window.at[centre, theirs]
            wait_bytes(piece, gather_recv.at[k - 1])
            to_neighbours(piece, theirs)

    loads[8].wait()

    def term(sibling, height):
        return rows_by_rows(
            in_half(sibling, side_at(height)), twice(top_couplings[height - 1])
        )

    terms = []
    for height in range(1, plane_levels + 1):
        first = sibling_start(place, height)
        sibling = sum(
            arrived_1[first + i].astype(F32)[:, : 2 * rank] for i in range(1 << height - 1)
        )
        terms.append(term(sibling, height))

    above = planes - 1 - level + len(steps) - behind

    @pl.when(above > 0)
    def _():
        pl.semaphore_wait(ready, above)

    for height in range(column_levels, 0, -1):
        pl.when(side_at(plane_levels + height) == 0)(functools.partial(send_column, height))
    for i in range(len(offsets)):
        early = far_goes_early(i)
        if early is not None:
            pl.when(jnp.logical_not(early))(functools.partial(send_far, i))

    loads[5].wait()
    loads[6].wait()

    @pl.when(device > 0)
    def _():
        wait_bytes(window.at[before], side_recv.at[0])

    @pl.when(device + 1 < n_leaf)
    def _():
        wait_bytes(window.at[after], side_recv.at[1])

    slots = blocks.shape[0]
    first_leaf = (device - 1) * leaves
    width = NEAR_CHUNK * leaf_size
    for chunk in range(leaves // NEAR_CHUNK):
        for leaf in range(chunk * NEAR_CHUNK, (chunk + 1) * NEAR_CHUNK):
            sources = jnp.concatenate(
                [
                    window[(src_s[q, leaf] - first_leaf) & (window.shape[0] - 1)]
                    for q in range(slots)
                ],
                axis=1,
            )
            matrix = jnp.concatenate([blocks[q, leaf] for q in range(slots)], axis=1)
            partial[:, leaf * leaf_size : (leaf + 1) * leaf_size] = rows_by_rows(
                sources, matrix
            ).astype(BF16)
        cols = pl.ds(chunk * width, width)
        for k in (2, 1, 3):
            if k < n_rhs:
                target = lax.rem(row + k, n_rhs)
                theirs = pl.ds(pl.multiple_of(target * vecs, vecs), vecs)
                send(
                    partial.at[theirs, cols],
                    others.at[k - 1, :, cols],
                    part_send,
                    part_recv,
                    device,
                    target,
                )

    loads[4].wait()
    loads[7].wait()
    wait_bytes(staged, far_recv)
    far = couplings.shape[2] // rank

    def far_block(leaf, f):
        return pool[far_s[f, leaf]].astype(F32)

    def far_row(leaf):
        return jnp.concatenate(
            [
                jnp.where(low, far_block(leaf, f), far_block(leaf, f + 1)).astype(BF16)
                for f in range(0, far, 2)
            ],
            axis=1,
        )

    for c in range(leaves // 2):
        sources = jnp.concatenate([far_row(2 * c), far_row(2 * c + 1)], axis=0)
        coupled[c] = both(rows_by_rows(sources, pair_of(couplings, 2 * c)))

    wait_bytes(others, part_recv)
    for leaf in range(leaves):
        cols = slice(leaf * leaf_size, (leaf + 1) * leaf_size)
        total = partial[my_rows, cols].astype(F32)
        for k in range(n_rhs - 1):
            total = total + others[k, :, cols].astype(F32)
        out[:, cols] = total

    wait_bytes(arrived_2.at[pl.ds(0, planes - 1)], recv_2)
    for height in range(1, column_levels + 1):
        first = sibling_start(level, height)
        sibling = sum(arrived_2[first + i].astype(F32) for i in range(1 << height - 1))
        terms.append(term(sibling, plane_levels + height))
    down = in_half(terms[top_levels - 1], side_at(top_levels))
    for height in range(top_levels - 1, 0, -1):
        spread = rows_by_cols(down, twice(top_moves[height - 1]))
        down = in_half(terms[height - 1] + spread, side_at(height))

    def split(pair):
        return jnp.concatenate(
            [jnp.where(low, pair, 0.0), jnp.where(low, 0.0, pair)], axis=0
        ).astype(BF16)

    pairs = [rows_by_cols(down, twice(moves[start]))]
    while len(pairs) < leaves // 2:
        start -= 2 * len(pairs)
        spreads = [
            rows_by_cols(split(pair), pair_of(moves, start + 2 * c))
            for c, pair in enumerate(pairs)
        ]
        pairs = [half for both_now in spreads for half in (both_now[:vecs], both_now[vecs:])]

    for c, pair in enumerate(pairs):
        far_part = rows_by_cols(split(pair + coupled[c]), pair_of(bases, 2 * c))
        for leaf, value in ((2 * c, far_part[:vecs]), (2 * c + 1, far_part[vecs:])):
            cols = slice(leaf * leaf_size, (leaf + 1) * leaf_size)
            out[:, cols] = out[:, cols] + value

    if n_rhs > 1:
        wait_bytes(others, gather_send)
        wait_bytes(others, part_send)

    @pl.when(device + 1 < n_leaf)
    def _():
        wait_bytes(window.at[before], side_send.at[0])

    @pl.when(device > 0)
    def _():
        wait_bytes(window.at[after], side_send.at[1])

    wait_bytes(staged, far_send)
    wait_bytes(arrived_1.at[pl.ds(0, plane - 1)], send_1)
    wait_bytes(arrived_2.at[pl.ds(0, planes - 1)], send_2)


def local(n_leaf, n_rhs, plane, *arrays):
    (vectors, near_blocks, near_src, basis, local_transfer, leaf_coupling, far_slot) = arrays[:7]
    want_leaf, top_transfer, top_coupling = arrays[7:]
    vecs, span = vectors.shape
    leaves, rank, leaf_size = basis.shape
    far_slot = far_slot.T
    planes = n_leaf // plane
    levels = plane.bit_length() - 1, planes.bit_length() - 1
    dma = pltpu.SemaphoreType.DMA
    scratch = [
        pltpu.VMEM((vecs, span), BF16),
        pltpu.VMEM((leaves, vecs, leaf_size), BF16),
        pltpu.VMEM((4 * leaves, n_rhs * vecs, leaf_size), BF16),
        pltpu.VMEM(near_blocks.shape, BF16),
        pltpu.VMEM(basis.shape, BF16),
        pltpu.VMEM(local_transfer.shape, BF16),
        pltpu.VMEM(leaf_coupling.shape, BF16),
        pltpu.VMEM(top_transfer.shape[1:], BF16),
        pltpu.VMEM(top_coupling.shape[1:], BF16),
        pltpu.SMEM(near_src.shape, jnp.int32),
        pltpu.SMEM(far_slot.shape, jnp.int32),
        pltpu.SMEM((7, n_leaf), jnp.int32),
        pltpu.VMEM((leaves, vecs, 2 * rank), BF16),
        pltpu.VMEM((leaves + n_leaf, vecs, 2 * rank), BF16),
        pltpu.VMEM((7, vecs, 2 * rank), BF16),
        pltpu.VMEM((levels[0], vecs, 4 * rank), BF16),
        pltpu.VMEM((plane, vecs, 4 * rank), BF16),
        pltpu.VMEM((levels[1], vecs, 2 * rank), BF16),
        pltpu.VMEM((planes, vecs, 2 * rank), BF16),
        pltpu.VMEM((leaves // 2, vecs, 2 * rank), F32),
        pltpu.VMEM((n_rhs * vecs, span), BF16),
        pltpu.VMEM((max(n_rhs - 1, 1), vecs, span), BF16),
        dma((9,)),
        dma((7,)),
        dma,
        dma((max(n_rhs - 1, 1),)),
        dma((2,)),
        dma((2,)),
        dma,
        dma,
        dma,
        dma,
        dma,
        dma,
        dma,
        dma,
        pltpu.SemaphoreType.REGULAR,
    ]
    return pl.pallas_call(
        functools.partial(kernel, n_leaf, n_rhs, plane),
        out_shape=pltpu.VMEM((vecs, span), F32),
        in_specs=[pl.BlockSpec(memory_space=pltpu.HBM)] * 10,
        out_specs=pl.BlockSpec(memory_space=pltpu.VMEM),
        scratch_shapes=scratch,
        compiler_params=pltpu.CompilerParams(
            collective_id=0, has_side_effects=True, vmem_limit_bytes=60 << 20
        ),
        name="hierarchical_product",
    )(
        vectors,
        near_blocks,
        near_src,
        basis,
        local_transfer,
        leaf_coupling,
        far_slot,
        want_leaf,
        top_transfer,
        top_coupling,
    )


def solution(mesh):
    in_specs = (
        P("rhs", "leaf"),
        P("rhs", "leaf", None, None),
        P("rhs", "leaf"),
        P("leaf", None, None),
        P("leaf", None, None),
        P("leaf", None, None),
        P("leaf", None),
        P(),
        P("leaf", None, None, None),
        P("leaf", None, None, None),
    )
    body = functools.partial(local, mesh.shape["leaf"], mesh.shape["rhs"], 8)
    return jax.shard_map(
        body, mesh=mesh, in_specs=in_specs, out_specs=P("rhs", "leaf"), check_vma=False
    )
```

```python
import functools

import jax
import jax.numpy as jnp
from jax import lax
from jax.experimental import pallas as pl
from jax.experimental.pallas import tpu as pltpu
from jax.sharding import PartitionSpec as P

MESH = pl.DeviceIdType.MESH
F32 = jnp.float32
BF16 = jnp.bfloat16
NEAR_CHUNK = 4


def rows_by_rows(lhs, rhs):
    return lax.dot_general(lhs, rhs, (((1,), (1,)), ((), ())), preferred_element_type=F32)


def rows_by_cols(lhs, rhs):
    return lax.dot_general(lhs, rhs, (((1,), (0,)), ((), ())), preferred_element_type=F32)


def twice(matrix):
    return jnp.concatenate([matrix, matrix], axis=0)


def kernel(
    n_leaf,
    n_rhs,
    plane,
    vectors,
    near_blocks,
    near_src,
    basis,
    local_transfer,
    leaf_coupling,
    far_slot,
    want_leaf,
    top_transfer,
    top_coupling,
    out,
    own,
    mine,
    window,
    blocks,
    bases,
    moves,
    couplings,
    top_moves,
    top_couplings,
    src_s,
    far_s,
    want_s,
    leaf_up,
    pool,
    staged,
    message_1,
    arrived_1,
    message_2,
    arrived_2,
    coupled,
    wide,
    partial,
    others,
    load_sem,
    want_sem,
    gather_send,
    gather_recv,
    side_send,
    side_recv,
    far_send,
    far_recv,
    send_1,
    recv_1,
    send_2,
    recv_2,
    part_send,
    part_recv,
    ready,
):
    vecs, span = vectors.shape
    leaves, rank, leaf_size = basis.shape
    device = lax.axis_index("leaf")
    row = lax.axis_index("rhs")
    planes = n_leaf // plane
    place = lax.rem(device, plane)
    level = lax.div(device, plane)
    offsets = [1, 2, 3, n_leaf - 1, n_leaf - 2, n_leaf - 3, n_leaf // 2]
    my_rows = pl.ds(pl.multiple_of(row * vecs, vecs), vecs)

    def leaf_at(offset):
        return lax.rem(device + offset, n_leaf)

    def in_plane(where):
        return level * plane + where

    def in_column(where):
        return where * plane + place

    loads = [
        pltpu.make_async_copy(vectors, own, load_sem.at[0]),
        pltpu.make_async_copy(basis, bases, load_sem.at[1]),
        pltpu.make_async_copy(local_transfer, moves, load_sem.at[2]),
        pltpu.make_async_copy(top_transfer.at[0], top_moves, load_sem.at[3]),
        pltpu.make_async_copy(far_slot, far_s, load_sem.at[4]),
        pltpu.make_async_copy(near_src, src_s, load_sem.at[5]),
        pltpu.make_async_copy(near_blocks, blocks, load_sem.at[6]),
        pltpu.make_async_copy(leaf_coupling, couplings, load_sem.at[7]),
        pltpu.make_async_copy(top_coupling.at[0], top_couplings, load_sem.at[8]),
    ]
    wants = [
        pltpu.make_async_copy(
            want_leaf.at[pl.ds(leaf_at(offset), 1)], want_s.at[pl.ds(i, 1)], want_sem.at[i]
        )
        for i, offset in enumerate(offsets)
    ]
    for load in loads + wants:
        load.start()

    barrier = pltpu.get_barrier_semaphore()

    def greet(leaf_index, rhs_index):
        pl.semaphore_signal(
            barrier, inc=1, device_id=(leaf_index, rhs_index), device_id_type=MESH
        )

    def loop(first, last, step):
        def body(i, carry):
            step(i)
            return carry

        lax.fori_loop(first, last, body, 0)

    steps = range(1, 4)
    for k in range(1, n_rhs):
        greet(device, lax.rem(row + k, n_rhs))
    for k in range(1, plane):
        greet(in_plane(lax.rem(place + k, plane)), row)
    for k in steps:
        greet(leaf_at(n_leaf - k), row)
        pl.when(device + k < n_leaf)(functools.partial(greet, leaf_at(k), row))
    loop(level + 1, planes, lambda other: greet(in_column(other), row))
    behind = sum((device >= k).astype(jnp.int32) for k in steps)
    greetings = (n_rhs - 1) + (plane - 1) + len(steps) + behind + level

    def send(src, dst, send_sem, recv_sem, leaf_index, rhs_index):
        pltpu.make_async_remote_copy(
            src_ref=src,
            dst_ref=dst,
            send_sem=send_sem,
            recv_sem=recv_sem,
            device_id=(leaf_index, rhs_index),
            device_id_type=MESH,
        ).start()

    def wait_bytes(ref, sem):
        pltpu.make_async_copy(ref, ref, sem).wait()

    lanes = lax.broadcasted_iota(jnp.int32, (vecs, 2 * rank), 1)
    low = lanes < rank

    def high_lanes(value):
        return lax.broadcasted_iota(jnp.int32, value.shape, 1) >= rank

    def in_half(value, side):
        return jnp.where(high_lanes(value) == (side == 1), value, 0.0).astype(BF16)

    def both(product):
        return jnp.where(low, product[:vecs], product[vecs:])

    def pair_of(ref, node):
        return ref[node : node + 2].reshape(2 * rank, -1)

    loads[0].wait()
    points = [own[:, t * leaf_size : (t + 1) * leaf_size] for t in range(leaves)]
    loads[1].wait()
    ups = []
    for c in range(leaves // 2):
        rows = jnp.concatenate([points[2 * c], points[2 * c + 1]], axis=0)
        ups.append(both(rows_by_rows(rows, pair_of(bases, 2 * c))))
    pairs = [pair.astype(BF16) for pair in ups]
    loads[2].wait()
    start = 0
    while len(pairs) > 1:
        nodes = len(pairs)
        pairs = [
            both(
                rows_by_rows(
                    jnp.concatenate([pairs[c], pairs[c + 1]], axis=0), pair_of(moves, start + c)
                )
            ).astype(BF16)
            for c in range(0, nodes, 2)
        ]
        start += nodes
    root = rows_by_rows(pairs[0], twice(moves[start]))

    loads[3].wait()
    plane_levels = plane.bit_length() - 1
    column_levels = planes.bit_length() - 1
    top_levels = plane_levels + column_levels

    def side_at(height):
        return lax.rem(lax.div(device, 1 << height - 1), 2)

    def lifted(value, height):
        return rows_by_rows(in_half(value, side_at(height)), twice(top_moves[height - 1]))

    def sibling_start(position, height):
        width = 1 << height - 1
        block = lax.div(position, width)
        return (block + 1 - 2 * lax.rem(block, 2)) * width

    shares = [root]
    for height in range(1, plane_levels + 1):
        shares.append(lifted(shares[-1], height))
    whole_share = shares[plane_levels].astype(BF16)
    for height in range(1, plane_levels + 1):
        message_1[height - 1] = jnp.concatenate(
            [shares[height - 1].astype(BF16), whole_share], axis=1
        )
    arrived_1[place] = message_1[0]

    pl.semaphore_wait(barrier, greetings)
    for height in range(plane_levels, 0, -1):
        for i in range(1 << height - 1):
            send(
                message_1.at[height - 1],
                arrived_1.at[place],
                send_1,
                recv_1,
                in_plane(sibling_start(place, height) + i),
                row,
            )

    def tell(other):
        pl.semaphore_signal(
            ready, inc=1, device_id=(in_column(other), row), device_id_type=MESH
        )

    loop(0, level, tell)
    for k in steps:

        @pl.when(device + k >= n_leaf)
        def _(k=k):
            pl.semaphore_signal(
                ready, inc=1, device_id=(leaf_at(k), row), device_id_type=MESH
            )

    for t in range(leaves):
        mine[t] = points[t]
        window[leaves + t, my_rows] = points[t]
    before, centre, after = (pl.ds(i * leaves, leaves) for i in range(3))
    for k in (2, 1, 3):
        if k < n_rhs:
            send(
                mine,
                window.at[centre, my_rows],
                gather_send,
                gather_recv.at[k - 1],
                device,
                lax.rem(row + k, n_rhs),
            )

    def to_neighbours(piece, rows):
        @pl.when(device + 1 < n_leaf)
        def _():
            send(
                piece, window.at[before, rows], side_send.at[0], side_recv.at[0], leaf_at(1), row
            )

        @pl.when(device > 0)
        def _():
            send(
                piece,
                window.at[after, rows],
                side_send.at[1],
                side_recv.at[1],
                leaf_at(n_leaf - 1),
                row,
            )

    to_neighbours(mine, my_rows)

    for c, pair in enumerate(ups):
        turned = pltpu.roll(pair, rank, 1)
        for leaf, value in (
            (2 * c, jnp.where(low, pair, turned).astype(BF16)),
            (2 * c + 1, jnp.where(low, turned, pair).astype(BF16)),
        ):
            leaf_up[leaf] = value
            pool[leaf] = value

    def send_far(i):
        send(
            staged.at[i],
            pool.at[leaves + device],
            far_send,
            far_recv,
            leaf_at(offsets[i]),
            row,
        )

    def far_goes_early(i):
        offset = offsets[i]
        if offset <= 3:
            return None
        return device >= n_leaf - offset

    for i, offset in enumerate(offsets):
        wants[i].wait()
        staged[i] = leaf_up[want_s[i, device]]
        early = far_goes_early(i)
        if early is None:
            send_far(i)
        else:
            pl.when(early)(functools.partial(send_far, i))

    wait_bytes(arrived_1.at[pl.ds(0, plane - 1)], recv_1)
    plane_up = sum(arrived_1[i].astype(F32)[:, 2 * rank :] for i in range(plane))
    share = plane_up
    for height in range(plane_levels + 1, top_levels + 1):
        if height > plane_levels + 1:
            share = lifted(share, height - 1)
        message_2[height - plane_levels - 1] = share.astype(BF16)

    def send_column(height):
        first = sibling_start(level, height)

        def one(i):
            send(
                message_2.at[height - 1],
                arrived_2.at[level],
                send_2,
                recv_2,
                in_column(first + i),
                row,
            )

        loop(0, 1 << height - 1, one)

    for height in range(column_levels, 0, -1):
        pl.when(side_at(plane_levels + height) == 1)(functools.partial(send_column, height))

    for k in (1, 3, 2):
        if k < n_rhs:
            theirs = pl.ds(pl.multiple_of(lax.rem(row + n_rhs - k, n_rhs) * vecs, vecs), vecs)
            piece = window.at[centre, theirs]
            wait_bytes(piece, gather_recv.at[k - 1])
            to_neighbours(piece, theirs)

    loads[8].wait()

    def term(sibling, height):
        return rows_by_rows(
            in_half(sibling, side_at(height)), twice(top_couplings[height - 1])
        )

    def split(pair):
        high = high_lanes(pair)
        return jnp.concatenate(
            [jnp.where(high, 0.0, pair), jnp.where(high, pair, 0.0)], axis=0
        ).astype(BF16)

    unit_rows = lax.broadcasted_iota(jnp.int32, (rank, 2 * rank), 0)
    unit_lanes = lax.broadcasted_iota(jnp.int32, (rank, 2 * rank), 1)
    unit = jnp.where((unit_lanes == unit_rows) | (unit_lanes == unit_rows + rank), 1.0, 0.0)
    down = in_half(term(unit, top_levels), side_at(top_levels))
    for height in range(top_levels - 1, 0, -1):
        spread = rows_by_cols(down, twice(top_moves[height - 1]))
        if height > plane_levels:
            spread = jnp.concatenate([term(unit, height), spread], axis=0)
        else:
            first = sibling_start(place, height)
            sibling = sum(
                arrived_1[first + i].astype(F32)[:, : 2 * rank] for i in range(1 << height - 1)
            )
            own_term = term(sibling, height)
            if height == plane_levels:
                spread = jnp.concatenate([own_term, spread], axis=0)
            else:
                spread = jnp.concatenate([spread[:vecs] + own_term, spread[vecs:]], axis=0)
        down = in_half(spread, side_at(height))
    pairs = [rows_by_cols(down, twice(moves[start]))]
    rows_now = pairs[0].shape[0]
    while len(pairs) < leaves // 2:
        start -= 2 * len(pairs)
        spreads = [
            rows_by_cols(split(pair), pair_of(moves, start + 2 * c))
            for c, pair in enumerate(pairs)
        ]
        pairs = [half for both_now in spreads for half in (both_now[:rows_now], both_now[rows_now:])]
    for c, pair in enumerate(pairs):
        coupled[c] = pair[:vecs]
        wide[c] = pair[vecs:].astype(BF16)

    above = planes - 1 - level + len(steps) - behind

    def send_above():
        @pl.when(above > 0)
        def _():
            pl.semaphore_wait(ready, above)

        for height in range(column_levels, 0, -1):
            pl.when(side_at(plane_levels + height) == 0)(functools.partial(send_column, height))
        for i in range(len(offsets)):
            early = far_goes_early(i)
            if early is not None:
                pl.when(jnp.logical_not(early))(functools.partial(send_far, i))

    upper_half = level >= planes // 2
    pl.when(upper_half)(send_above)

    loads[5].wait()
    loads[6].wait()

    @pl.when(device > 0)
    def _():
        wait_bytes(window.at[before], side_recv.at[0])

    @pl.when(device + 1 < n_leaf)
    def _():
        wait_bytes(window.at[after], side_recv.at[1])

    slots = blocks.shape[0]
    first_leaf = (device - 1) * leaves
    width = NEAR_CHUNK * leaf_size
    for chunk in range(leaves // NEAR_CHUNK):
        for leaf in range(chunk * NEAR_CHUNK, (chunk + 1) * NEAR_CHUNK):
            sources = jnp.concatenate(
                [
                    window[(src_s[q, leaf] - first_leaf) & (window.shape[0] - 1)]
                    for q in range(slots)
                ],
                axis=1,
            )
            matrix = jnp.concatenate([blocks[q, leaf] for q in range(slots)], axis=1)
            partial[:, leaf * leaf_size : (leaf + 1) * leaf_size] = rows_by_rows(
                sources, matrix
            ).astype(BF16)
        cols = pl.ds(chunk * width, width)
        for k in (2, 1, 3):
            if k < n_rhs:
                target = lax.rem(row + k, n_rhs)
                theirs = pl.ds(pl.multiple_of(target * vecs, vecs), vecs)
                send(
                    partial.at[theirs, cols],
                    others.at[k - 1, :, cols],
                    part_send,
                    part_recv,
                    device,
                    target,
                )

    pl.when(jnp.logical_not(upper_half))(send_above)

    loads[4].wait()
    loads[7].wait()
    wait_bytes(staged, far_recv)
    far = couplings.shape[2] // rank

    def far_block(leaf, f):
        return pool[far_s[f, leaf]].astype(F32)

    def far_row(leaf):
        return jnp.concatenate(
            [
                jnp.where(low, far_block(leaf, f), far_block(leaf, f + 1)).astype(BF16)
                for f in range(0, far, 2)
            ],
            axis=1,
        )

    for c in range(leaves // 2):
        sources = jnp.concatenate([far_row(2 * c), far_row(2 * c + 1)], axis=0)
        coupled[c] = coupled[c] + both(rows_by_rows(sources, pair_of(couplings, 2 * c)))

    def add_near():
        wait_bytes(others, part_recv)
        for leaf in range(leaves):
            cols = slice(leaf * leaf_size, (leaf + 1) * leaf_size)
            total = out[:, cols] + partial[my_rows, cols].astype(F32)
            for k in range(n_rhs - 1):
                total = total + others[k, :, cols].astype(F32)
            out[:, cols] = total

    out[...] = jnp.zeros_like(out)
    pl.when(jnp.logical_not(upper_half))(add_near)

    wait_bytes(arrived_2.at[pl.ds(0, planes - 1)], recv_2)
    siblings = []
    for height in range(1, column_levels + 1):
        first = sibling_start(level, height)
        siblings.append(sum(arrived_2[first + i].astype(F32) for i in range(1 << height - 1)))
    siblings = jnp.concatenate(
        [jnp.where(low, *siblings[i : i + 2]) for i in range(0, column_levels, 2)], axis=1
    ).astype(BF16)
    for c in range(leaves // 2):
        pair = coupled[c] + rows_by_cols(siblings, wide[c])
        far_part = rows_by_cols(split(pair), pair_of(bases, 2 * c))
        for leaf, value in ((2 * c, far_part[:vecs]), (2 * c + 1, far_part[vecs:])):
            cols = slice(leaf * leaf_size, (leaf + 1) * leaf_size)
            out[:, cols] = out[:, cols] + value

    pl.when(upper_half)(add_near)

    if n_rhs > 1:
        wait_bytes(others, gather_send)
        wait_bytes(others, part_send)

    @pl.when(device + 1 < n_leaf)
    def _():
        wait_bytes(window.at[before], side_send.at[0])

    @pl.when(device > 0)
    def _():
        wait_bytes(window.at[after], side_send.at[1])

    wait_bytes(staged, far_send)
    wait_bytes(arrived_1.at[pl.ds(0, plane - 1)], send_1)
    wait_bytes(arrived_2.at[pl.ds(0, planes - 1)], send_2)


def local(n_leaf, n_rhs, plane, *arrays):
    (vectors, near_blocks, near_src, basis, local_transfer, leaf_coupling, far_slot) = arrays[:7]
    want_leaf, top_transfer, top_coupling = arrays[7:]
    vecs, span = vectors.shape
    leaves, rank, leaf_size = basis.shape
    far_slot = far_slot.T
    planes = n_leaf // plane
    levels = plane.bit_length() - 1, planes.bit_length() - 1
    dma = pltpu.SemaphoreType.DMA
    scratch = [
        pltpu.VMEM((vecs, span), BF16),
        pltpu.VMEM((leaves, vecs, leaf_size), BF16),
        pltpu.VMEM((4 * leaves, n_rhs * vecs, leaf_size), BF16),
        pltpu.VMEM(near_blocks.shape, BF16),
        pltpu.VMEM(basis.shape, BF16),
        pltpu.VMEM(local_transfer.shape, BF16),
        pltpu.VMEM(leaf_coupling.shape, BF16),
        pltpu.VMEM(top_transfer.shape[1:], BF16),
        pltpu.VMEM(top_coupling.shape[1:], BF16),
        pltpu.SMEM(near_src.shape, jnp.int32),
        pltpu.SMEM(far_slot.shape, jnp.int32),
        pltpu.SMEM((7, n_leaf), jnp.int32),
        pltpu.VMEM((leaves, vecs, 2 * rank), BF16),
        pltpu.VMEM((leaves + n_leaf, vecs, 2 * rank), BF16),
        pltpu.VMEM((7, vecs, 2 * rank), BF16),
        pltpu.VMEM((levels[0], vecs, 4 * rank), BF16),
        pltpu.VMEM((plane, vecs, 4 * rank), BF16),
        pltpu.VMEM((levels[1], vecs, 2 * rank), BF16),
        pltpu.VMEM((planes, vecs, 2 * rank), BF16),
        pltpu.VMEM((leaves // 2, vecs, 2 * rank), F32),
        pltpu.VMEM((leaves // 2, levels[1] * rank, 2 * rank), BF16),
        pltpu.VMEM((n_rhs * vecs, span), BF16),
        pltpu.VMEM((max(n_rhs - 1, 1), vecs, span), BF16),
        dma((9,)),
        dma((7,)),
        dma,
        dma((max(n_rhs - 1, 1),)),
        dma((2,)),
        dma((2,)),
        dma,
        dma,
        dma,
        dma,
        dma,
        dma,
        dma,
        dma,
        pltpu.SemaphoreType.REGULAR,
    ]
    return pl.pallas_call(
        functools.partial(kernel, n_leaf, n_rhs, plane),
        out_shape=pltpu.VMEM((vecs, span), F32),
        in_specs=[pl.BlockSpec(memory_space=pltpu.HBM)] * 10,
        out_specs=pl.BlockSpec(memory_space=pltpu.VMEM),
        scratch_shapes=scratch,
        compiler_params=pltpu.CompilerParams(
            collective_id=0, has_side_effects=True, vmem_limit_bytes=60 << 20
        ),
        name="hierarchical_product",
    )(
        vectors,
        near_blocks,
        near_src,
        basis,
        local_transfer,
        leaf_coupling,
        far_slot,
        want_leaf,
        top_transfer,
        top_coupling,
    )


def solution(mesh):
    in_specs = (
        P("rhs", "leaf"),
        P("rhs", "leaf", None, None),
        P("rhs", "leaf"),
        P("leaf", None, None),
        P("leaf", None, None),
        P("leaf", None, None),
        P("leaf", None),
        P(),
        P("leaf", None, None, None),
        P("leaf", None, None, None),
    )
    body = functools.partial(local, mesh.shape["leaf"], mesh.shape["rhs"], 8)
    return jax.shard_map(
        body, mesh=mesh, in_specs=in_specs, out_specs=P("rhs", "leaf"), check_vma=False
    )
```

```python
import functools

import jax
import jax.numpy as jnp
from jax import lax
from jax.experimental import pallas as pl
from jax.experimental.pallas import tpu as pltpu
from jax.sharding import PartitionSpec as P

MESH = pl.DeviceIdType.MESH
F32 = jnp.float32
BF16 = jnp.bfloat16
NEAR_CHUNK = 4


def rows_by_rows(lhs, rhs):
    return lax.dot_general(lhs, rhs, (((1,), (1,)), ((), ())), preferred_element_type=F32)


def rows_by_cols(lhs, rhs):
    return lax.dot_general(lhs, rhs, (((1,), (0,)), ((), ())), preferred_element_type=F32)


def twice(matrix):
    return jnp.concatenate([matrix, matrix], axis=0)


def kernel(
    n_leaf,
    n_rhs,
    plane,
    vectors,
    near_blocks,
    near_src,
    basis,
    local_transfer,
    leaf_coupling,
    far_slot,
    want_leaf,
    top_transfer,
    top_coupling,
    out,
    own,
    mine,
    window,
    blocks,
    bases,
    moves,
    couplings,
    top_moves,
    top_couplings,
    src_s,
    far_s,
    want_s,
    leaf_up,
    pool,
    staged,
    message_1,
    arrived_1,
    message_2,
    arrived_2,
    coupled,
    wide,
    partial,
    others,
    load_sem,
    want_sem,
    gather_send,
    gather_recv,
    side_send,
    side_recv,
    far_send,
    far_recv,
    send_1,
    recv_1,
    send_2,
    recv_2,
    part_send,
    part_recv,
    ready,
):
    vecs, span = vectors.shape
    leaves, rank, leaf_size = basis.shape
    device = lax.axis_index("leaf")
    row = lax.axis_index("rhs")
    planes = n_leaf // plane
    place = lax.rem(device, plane)
    level = lax.div(device, plane)
    offsets = [1, 2, 3, n_leaf - 1, n_leaf - 2, n_leaf - 3, n_leaf // 2]
    my_rows = pl.ds(pl.multiple_of(row * vecs, vecs), vecs)

    def leaf_at(offset):
        return lax.rem(device + offset, n_leaf)

    def in_plane(where):
        return level * plane + where

    def in_column(where):
        return where * plane + place

    loads = [
        pltpu.make_async_copy(vectors, own, load_sem.at[0]),
        pltpu.make_async_copy(basis, bases, load_sem.at[1]),
        pltpu.make_async_copy(local_transfer, moves, load_sem.at[2]),
        pltpu.make_async_copy(top_transfer.at[0], top_moves, load_sem.at[3]),
        pltpu.make_async_copy(far_slot, far_s, load_sem.at[4]),
        pltpu.make_async_copy(near_src, src_s, load_sem.at[5]),
        pltpu.make_async_copy(near_blocks, blocks, load_sem.at[6]),
        pltpu.make_async_copy(leaf_coupling, couplings, load_sem.at[7]),
        pltpu.make_async_copy(top_coupling.at[0], top_couplings, load_sem.at[8]),
    ]
    wants = [
        pltpu.make_async_copy(
            want_leaf.at[pl.ds(leaf_at(offset), 1)], want_s.at[pl.ds(i, 1)], want_sem.at[i]
        )
        for i, offset in enumerate(offsets)
    ]
    for load in loads[:4]:
        load.start()

    barrier = pltpu.get_barrier_semaphore()

    def greet(leaf_index, rhs_index):
        pl.semaphore_signal(
            barrier, inc=1, device_id=(leaf_index, rhs_index), device_id_type=MESH
        )

    def loop(first, last, step):
        def body(i, carry):
            step(i)
            return carry

        lax.fori_loop(first, last, body, 0)

    steps = range(1, 4)
    for k in range(1, n_rhs):
        greet(device, lax.rem(row + k, n_rhs))
    for k in range(1, plane):
        greet(in_plane(lax.rem(place + k, plane)), row)
    for k in steps:
        greet(leaf_at(n_leaf - k), row)
        pl.when(device + k < n_leaf)(functools.partial(greet, leaf_at(k), row))
    loop(level + 1, planes, lambda other: greet(in_column(other), row))
    behind = sum((device >= k).astype(jnp.int32) for k in steps)
    greetings = (n_rhs - 1) + (plane - 1) + len(steps) + behind + level

    def send(src, dst, send_sem, recv_sem, leaf_index, rhs_index):
        pltpu.make_async_remote_copy(
            src_ref=src,
            dst_ref=dst,
            send_sem=send_sem,
            recv_sem=recv_sem,
            device_id=(leaf_index, rhs_index),
            device_id_type=MESH,
        ).start()

    def wait_bytes(ref, sem):
        pltpu.make_async_copy(ref, ref, sem).wait()

    lanes = lax.broadcasted_iota(jnp.int32, (vecs, 2 * rank), 1)
    low = lanes < rank

    def high_lanes(value):
        return lax.broadcasted_iota(jnp.int32, value.shape, 1) >= rank

    def in_half(value, side):
        return jnp.where(high_lanes(value) == (side == 1), value, 0.0).astype(BF16)

    def both(product):
        return jnp.where(low, product[:vecs], product[vecs:])

    def pair_of(ref, node):
        return ref[node : node + 2].reshape(2 * rank, -1)

    loads[0].wait()
    points = [own[:, t * leaf_size : (t + 1) * leaf_size] for t in range(leaves)]
    before, centre, after = (pl.ds(i * leaves, leaves) for i in range(3))

    def to_neighbours(piece, rows):
        @pl.when(device + 1 < n_leaf)
        def _():
            send(
                piece, window.at[before, rows], side_send.at[0], side_recv.at[0], leaf_at(1), row
            )

        @pl.when(device > 0)
        def _():
            send(
                piece,
                window.at[after, rows],
                side_send.at[1],
                side_recv.at[1],
                leaf_at(n_leaf - 1),
                row,
            )

    def spread_points():
        for t in range(leaves):
            mine[t] = points[t]
            window[leaves + t, my_rows] = points[t]
        for k in (2, 1, 3):
            if k < n_rhs:
                send(
                    mine,
                    window.at[centre, my_rows],
                    gather_send,
                    gather_recv.at[k - 1],
                    device,
                    lax.rem(row + k, n_rhs),
                )

        to_neighbours(mine, my_rows)

    upper_half = level >= planes // 2

    @pl.when(jnp.logical_not(upper_half))
    def _():
        pl.semaphore_wait(barrier, greetings)
        spread_points()

    loads[1].wait()
    ups = []
    for c in range(leaves // 2):
        rows = jnp.concatenate([points[2 * c], points[2 * c + 1]], axis=0)
        ups.append(both(rows_by_rows(rows, pair_of(bases, 2 * c))))
    pairs = [pair.astype(BF16) for pair in ups]
    loads[2].wait()
    start = 0
    while len(pairs) > 1:
        nodes = len(pairs)
        pairs = [
            both(
                rows_by_rows(
                    jnp.concatenate([pairs[c], pairs[c + 1]], axis=0), pair_of(moves, start + c)
                )
            ).astype(BF16)
            for c in range(0, nodes, 2)
        ]
        start += nodes
    root = rows_by_rows(pairs[0], twice(moves[start]))

    loads[3].wait()
    plane_levels = plane.bit_length() - 1
    column_levels = planes.bit_length() - 1
    top_levels = plane_levels + column_levels

    def side_at(height):
        return lax.rem(lax.div(device, 1 << height - 1), 2)

    def lifted(value, height):
        return rows_by_rows(in_half(value, side_at(height)), twice(top_moves[height - 1]))

    def sibling_start(position, height):
        width = 1 << height - 1
        block = lax.div(position, width)
        return (block + 1 - 2 * lax.rem(block, 2)) * width

    shares = [root]
    for height in range(1, plane_levels + 1):
        shares.append(lifted(shares[-1], height))
    whole_share = shares[plane_levels].astype(BF16)
    for height in range(1, plane_levels + 1):
        message_1[height - 1] = jnp.concatenate(
            [shares[height - 1].astype(BF16), whole_share], axis=1
        )
    arrived_1[place] = message_1[0]

    @pl.when(upper_half)
    def _():
        pl.semaphore_wait(barrier, greetings)

    for height in range(plane_levels, 0, -1):
        for i in range(1 << height - 1):
            send(
                message_1.at[height - 1],
                arrived_1.at[place],
                send_1,
                recv_1,
                in_plane(sibling_start(place, height) + i),
                row,
            )

    def tell(other):
        pl.semaphore_signal(
            ready, inc=1, device_id=(in_column(other), row), device_id_type=MESH
        )

    loop(0, level, tell)
    for k in steps:

        @pl.when(device + k >= n_leaf)
        def _(k=k):
            pl.semaphore_signal(
                ready, inc=1, device_id=(leaf_at(k), row), device_id_type=MESH
            )

    for load in wants + loads[4:]:
        load.start()

    pl.when(upper_half)(spread_points)

    for c, pair in enumerate(ups):
        turned = pltpu.roll(pair, rank, 1)
        for leaf, value in (
            (2 * c, jnp.where(low, pair, turned).astype(BF16)),
            (2 * c + 1, jnp.where(low, turned, pair).astype(BF16)),
        ):
            leaf_up[leaf] = value
            pool[leaf] = value

    def send_far(i):
        send(
            staged.at[i],
            pool.at[leaves + device],
            far_send,
            far_recv,
            leaf_at(offsets[i]),
            row,
        )

    def far_goes_early(i):
        offset = offsets[i]
        if offset <= 3:
            return None
        return device >= n_leaf - offset

    for i, offset in enumerate(offsets):
        wants[i].wait()
        staged[i] = leaf_up[want_s[i, device]]
        early = far_goes_early(i)
        if early is None:
            send_far(i)
        else:
            pl.when(early)(functools.partial(send_far, i))

    unit_rows = lax.broadcasted_iota(jnp.int32, (rank, 2 * rank), 0)
    unit_lanes = lax.broadcasted_iota(jnp.int32, (rank, 2 * rank), 1)
    unit = jnp.where((unit_lanes == unit_rows) | (unit_lanes == unit_rows + rank), 1.0, 0.0)
    lifts = [unit]
    for height in range(plane_levels + 1, top_levels):
        lifts.append(lifted(lifts[-1], height))
    lift = jnp.concatenate([each.astype(BF16) for each in lifts[1:]], axis=1)
    wait_bytes(arrived_1.at[pl.ds(0, plane - 1)], recv_1)
    plane_up = sum(arrived_1[i].astype(F32)[:, 2 * rank :] for i in range(plane)).astype(BF16)
    message_2[0] = plane_up
    above_plane = rows_by_cols(plane_up[:, :rank], lift).astype(BF16)
    for i in range(1, column_levels):
        message_2[i] = above_plane[:, (i - 1) * 2 * rank : i * 2 * rank]

    def send_column(height):
        first = sibling_start(level, height)

        def one(i):
            send(
                message_2.at[height - 1],
                arrived_2.at[level],
                send_2,
                recv_2,
                in_column(first + i),
                row,
            )

        loop(0, 1 << height - 1, one)

    for height in range(column_levels, 0, -1):
        pl.when(side_at(plane_levels + height) == 1)(functools.partial(send_column, height))

    for k in (1, 3, 2):
        if k < n_rhs:
            theirs = pl.ds(pl.multiple_of(lax.rem(row + n_rhs - k, n_rhs) * vecs, vecs), vecs)
            piece = window.at[centre, theirs]
            wait_bytes(piece, gather_recv.at[k - 1])
            to_neighbours(piece, theirs)

    loads[8].wait()

    def term(sibling, height):
        return rows_by_rows(
            in_half(sibling, side_at(height)), twice(top_couplings[height - 1])
        )

    def split(pair):
        high = high_lanes(pair)
        return jnp.concatenate(
            [jnp.where(high, 0.0, pair), jnp.where(high, pair, 0.0)], axis=0
        ).astype(BF16)

    down = in_half(term(unit, top_levels), side_at(top_levels))
    for height in range(top_levels - 1, 0, -1):
        spread = rows_by_cols(down, twice(top_moves[height - 1]))
        if height > plane_levels:
            spread = jnp.concatenate([term(unit, height), spread], axis=0)
        else:
            first = sibling_start(place, height)
            sibling = sum(
                arrived_1[first + i].astype(F32)[:, : 2 * rank] for i in range(1 << height - 1)
            )
            own_term = term(sibling, height)
            if height == plane_levels:
                spread = jnp.concatenate([own_term, spread], axis=0)
            else:
                spread = jnp.concatenate([spread[:vecs] + own_term, spread[vecs:]], axis=0)
        down = in_half(spread, side_at(height))
    pairs = [rows_by_cols(down, twice(moves[start]))]
    rows_now = pairs[0].shape[0]
    while len(pairs) < leaves // 2:
        start -= 2 * len(pairs)
        spreads = [
            rows_by_cols(split(pair), pair_of(moves, start + 2 * c))
            for c, pair in enumerate(pairs)
        ]
        pairs = [half for both_now in spreads for half in (both_now[:rows_now], both_now[rows_now:])]
    for c, pair in enumerate(pairs):
        coupled[c] = pair[:vecs]
        wide[c] = pair[vecs:].astype(BF16)

    above = planes - 1 - level + len(steps) - behind

    def send_above():
        @pl.when(above > 0)
        def _():
            pl.semaphore_wait(ready, above)

        for height in range(column_levels, 0, -1):
            pl.when(side_at(plane_levels + height) == 0)(functools.partial(send_column, height))
        for i in range(len(offsets)):
            early = far_goes_early(i)
            if early is not None:
                pl.when(jnp.logical_not(early))(functools.partial(send_far, i))

    early_planes = level < planes // 4
    pl.when(jnp.logical_not(early_planes))(send_above)

    loads[5].wait()
    loads[6].wait()

    @pl.when(device > 0)
    def _():
        wait_bytes(window.at[before], side_recv.at[0])

    @pl.when(device + 1 < n_leaf)
    def _():
        wait_bytes(window.at[after], side_recv.at[1])

    slots = blocks.shape[0]
    first_leaf = (device - 1) * leaves
    width = NEAR_CHUNK * leaf_size
    for chunk in range(leaves // NEAR_CHUNK):
        for leaf in range(chunk * NEAR_CHUNK, (chunk + 1) * NEAR_CHUNK):
            sources = jnp.concatenate(
                [
                    window[(src_s[q, leaf] - first_leaf) & (window.shape[0] - 1)]
                    for q in range(slots)
                ],
                axis=1,
            )
            matrix = jnp.concatenate([blocks[q, leaf] for q in range(slots)], axis=1)
            partial[:, leaf * leaf_size : (leaf + 1) * leaf_size] = rows_by_rows(
                sources, matrix
            ).astype(BF16)
        cols = pl.ds(chunk * width, width)
        for k in (2, 1, 3):
            if k < n_rhs:
                target = lax.rem(row + k, n_rhs)
                theirs = pl.ds(pl.multiple_of(target * vecs, vecs), vecs)
                send(
                    partial.at[theirs, cols],
                    others.at[k - 1, :, cols],
                    part_send,
                    part_recv,
                    device,
                    target,
                )

    pl.when(early_planes)(send_above)

    loads[4].wait()
    loads[7].wait()
    wait_bytes(staged, far_recv)
    far = couplings.shape[2] // rank

    def far_block(leaf, f):
        return pool[far_s[f, leaf]].astype(F32)

    def far_row(leaf):
        return jnp.concatenate(
            [
                jnp.where(low, far_block(leaf, f), far_block(leaf, f + 1)).astype(BF16)
                for f in range(0, far, 2)
            ],
            axis=1,
        )

    for c in range(leaves // 2):
        sources = jnp.concatenate([far_row(2 * c), far_row(2 * c + 1)], axis=0)
        coupled[c] = coupled[c] + both(rows_by_rows(sources, pair_of(couplings, 2 * c)))

    def add_near():
        wait_bytes(others, part_recv)
        for leaf in range(leaves):
            cols = slice(leaf * leaf_size, (leaf + 1) * leaf_size)
            total = out[:, cols] + partial[my_rows, cols].astype(F32)
            for k in range(n_rhs - 1):
                total = total + others[k, :, cols].astype(F32)
            out[:, cols] = total

    out[...] = jnp.zeros_like(out)
    pl.when(jnp.logical_not(upper_half))(add_near)

    wait_bytes(arrived_2.at[pl.ds(0, planes - 1)], recv_2)
    siblings = []
    for height in range(1, column_levels + 1):
        first = sibling_start(level, height)
        siblings.append(sum(arrived_2[first + i].astype(F32) for i in range(1 << height - 1)))
    siblings = jnp.concatenate(
        [jnp.where(low, *siblings[i : i + 2]) for i in range(0, column_levels, 2)], axis=1
    ).astype(BF16)
    for c in range(leaves // 2):
        pair = coupled[c] + rows_by_cols(siblings, wide[c])
        far_part = rows_by_cols(split(pair), pair_of(bases, 2 * c))
        for leaf, value in ((2 * c, far_part[:vecs]), (2 * c + 1, far_part[vecs:])):
            cols = slice(leaf * leaf_size, (leaf + 1) * leaf_size)
            out[:, cols] = out[:, cols] + value

    pl.when(upper_half)(add_near)

    if n_rhs > 1:
        wait_bytes(others, gather_send)
        wait_bytes(others, part_send)

    @pl.when(device + 1 < n_leaf)
    def _():
        wait_bytes(window.at[before], side_send.at[0])

    @pl.when(device > 0)
    def _():
        wait_bytes(window.at[after], side_send.at[1])

    wait_bytes(staged, far_send)
    wait_bytes(arrived_1.at[pl.ds(0, plane - 1)], send_1)
    wait_bytes(arrived_2.at[pl.ds(0, planes - 1)], send_2)


def local(n_leaf, n_rhs, plane, *arrays):
    (vectors, near_blocks, near_src, basis, local_transfer, leaf_coupling, far_slot) = arrays[:7]
    want_leaf, top_transfer, top_coupling = arrays[7:]
    vecs, span = vectors.shape
    leaves, rank, leaf_size = basis.shape
    far_slot = far_slot.T
    planes = n_leaf // plane
    levels = plane.bit_length() - 1, planes.bit_length() - 1
    dma = pltpu.SemaphoreType.DMA
    scratch = [
        pltpu.VMEM((vecs, span), BF16),
        pltpu.VMEM((leaves, vecs, leaf_size), BF16),
        pltpu.VMEM((4 * leaves, n_rhs * vecs, leaf_size), BF16),
        pltpu.VMEM(near_blocks.shape, BF16),
        pltpu.VMEM(basis.shape, BF16),
        pltpu.VMEM(local_transfer.shape, BF16),
        pltpu.VMEM(leaf_coupling.shape, BF16),
        pltpu.VMEM(top_transfer.shape[1:], BF16),
        pltpu.VMEM(top_coupling.shape[1:], BF16),
        pltpu.SMEM(near_src.shape, jnp.int32),
        pltpu.SMEM(far_slot.shape, jnp.int32),
        pltpu.SMEM((7, n_leaf), jnp.int32),
        pltpu.VMEM((leaves, vecs, 2 * rank), BF16),
        pltpu.VMEM((leaves + n_leaf, vecs, 2 * rank), BF16),
        pltpu.VMEM((7, vecs, 2 * rank), BF16),
        pltpu.VMEM((levels[0], vecs, 4 * rank), BF16),
        pltpu.VMEM((plane, vecs, 4 * rank), BF16),
        pltpu.VMEM((levels[1], vecs, 2 * rank), BF16),
        pltpu.VMEM((planes, vecs, 2 * rank), BF16),
        pltpu.VMEM((leaves // 2, vecs, 2 * rank), F32),
        pltpu.VMEM((leaves // 2, levels[1] * rank, 2 * rank), BF16),
        pltpu.VMEM((n_rhs * vecs, span), BF16),
        pltpu.VMEM((max(n_rhs - 1, 1), vecs, span), BF16),
        dma((9,)),
        dma((7,)),
        dma,
        dma((max(n_rhs - 1, 1),)),
        dma((2,)),
        dma((2,)),
        dma,
        dma,
        dma,
        dma,
        dma,
        dma,
        dma,
        dma,
        pltpu.SemaphoreType.REGULAR,
    ]
    return pl.pallas_call(
        functools.partial(kernel, n_leaf, n_rhs, plane),
        out_shape=pltpu.VMEM((vecs, span), F32),
        in_specs=[pl.BlockSpec(memory_space=pltpu.HBM)] * 10,
        out_specs=pl.BlockSpec(memory_space=pltpu.VMEM),
        scratch_shapes=scratch,
        compiler_params=pltpu.CompilerParams(
            collective_id=0, has_side_effects=True, vmem_limit_bytes=60 << 20
        ),
        name="hierarchical_product",
    )(
        vectors,
        near_blocks,
        near_src,
        basis,
        local_transfer,
        leaf_coupling,
        far_slot,
        want_leaf,
        top_transfer,
        top_coupling,
    )


def solution(mesh):
    in_specs = (
        P("rhs", "leaf"),
        P("rhs", "leaf", None, None),
        P("rhs", "leaf"),
        P("leaf", None, None),
        P("leaf", None, None),
        P("leaf", None, None),
        P("leaf", None),
        P(),
        P("leaf", None, None, None),
        P("leaf", None, None, None),
    )
    body = functools.partial(local, mesh.shape["leaf"], mesh.shape["rhs"], 8)
    return jax.shard_map(
        body, mesh=mesh, in_specs=in_specs, out_specs=P("rhs", "leaf"), check_vma=False
    )
```

```python
import functools

import jax
import jax.numpy as jnp
from jax import lax
from jax.experimental import pallas as pl
from jax.experimental.pallas import tpu as pltpu
from jax.sharding import PartitionSpec as P

MESH = pl.DeviceIdType.MESH
F32 = jnp.float32
BF16 = jnp.bfloat16
NEAR_CHUNK = 4


def rows_by_rows(lhs, rhs):
    return lax.dot_general(lhs, rhs, (((1,), (1,)), ((), ())), preferred_element_type=F32)


def rows_by_cols(lhs, rhs):
    return lax.dot_general(lhs, rhs, (((1,), (0,)), ((), ())), preferred_element_type=F32)


def twice(matrix):
    return jnp.concatenate([matrix, matrix], axis=0)


def kernel(
    n_leaf,
    n_rhs,
    plane,
    vectors,
    near_blocks,
    near_src,
    basis,
    local_transfer,
    leaf_coupling,
    far_slot,
    want_leaf,
    top_transfer,
    top_coupling,
    out,
    own,
    mine,
    window,
    blocks,
    bases,
    moves,
    couplings,
    top_moves,
    top_couplings,
    src_s,
    far_s,
    want_s,
    leaf_up,
    pool,
    staged,
    message_1,
    arrived_1,
    message_2,
    arrived_2,
    coupled,
    wide,
    partial,
    others,
    load_sem,
    want_sem,
    gather_send,
    gather_recv,
    side_send,
    side_recv,
    far_send,
    far_recv,
    send_1,
    recv_1,
    send_2,
    recv_2,
    part_send,
    part_recv,
    ready,
    row_ready,
):
    vecs, span = vectors.shape
    leaves, rank, leaf_size = basis.shape
    device = lax.axis_index("leaf")
    row = lax.axis_index("rhs")
    planes = n_leaf // plane
    place = lax.rem(device, plane)
    level = lax.div(device, plane)
    offsets = [1, 2, 3, n_leaf - 1, n_leaf - 2, n_leaf - 3, n_leaf // 2]
    my_rows = pl.ds(pl.multiple_of(row * vecs, vecs), vecs)

    def leaf_at(offset):
        return lax.rem(device + offset, n_leaf)

    def in_plane(where):
        return level * plane + where

    def in_column(where):
        return where * plane + place

    loads = [
        pltpu.make_async_copy(vectors, own, load_sem.at[0]),
        pltpu.make_async_copy(basis, bases, load_sem.at[1]),
        pltpu.make_async_copy(local_transfer, moves, load_sem.at[2]),
        pltpu.make_async_copy(top_transfer.at[0], top_moves, load_sem.at[3]),
        pltpu.make_async_copy(far_slot, far_s, load_sem.at[4]),
        pltpu.make_async_copy(near_src, src_s, load_sem.at[5]),
        pltpu.make_async_copy(near_blocks, blocks, load_sem.at[6]),
        pltpu.make_async_copy(leaf_coupling, couplings, load_sem.at[7]),
        pltpu.make_async_copy(top_coupling.at[0], top_couplings, load_sem.at[8]),
    ]
    wants = [
        pltpu.make_async_copy(
            want_leaf.at[pl.ds(leaf_at(offset), 1)], want_s.at[pl.ds(i, 1)], want_sem.at[i]
        )
        for i, offset in enumerate(offsets)
    ]
    for load in loads[:4]:
        load.start()

    barrier = pltpu.get_barrier_semaphore()

    def greet(leaf_index, rhs_index):
        pl.semaphore_signal(
            barrier, inc=1, device_id=(leaf_index, rhs_index), device_id_type=MESH
        )

    def loop(first, last, step):
        def body(i, carry):
            step(i)
            return carry

        lax.fori_loop(first, last, body, 0)

    steps = range(1, 4)
    for k in range(1, plane):
        greet(in_plane(lax.rem(place + k, plane)), row)
    for k in range(1, n_rhs):
        pl.when(row + k < n_rhs)(functools.partial(greet, device, row + k))
    for k in steps:
        greet(leaf_at(n_leaf - k), row)
        pl.when(device + k < n_leaf)(functools.partial(greet, leaf_at(k), row))
    loop(level + 1, planes, lambda other: greet(in_column(other), row))
    behind = sum((device >= k).astype(jnp.int32) for k in steps)
    greetings = row + (plane - 1) + len(steps) + behind + level

    def send(src, dst, send_sem, recv_sem, leaf_index, rhs_index):
        pltpu.make_async_remote_copy(
            src_ref=src,
            dst_ref=dst,
            send_sem=send_sem,
            recv_sem=recv_sem,
            device_id=(leaf_index, rhs_index),
            device_id_type=MESH,
        ).start()

    def wait_bytes(ref, sem):
        pltpu.make_async_copy(ref, ref, sem).wait()

    lanes = lax.broadcasted_iota(jnp.int32, (vecs, 2 * rank), 1)
    low = lanes < rank

    def high_lanes(value):
        return lax.broadcasted_iota(jnp.int32, value.shape, 1) >= rank

    def in_half(value, side):
        return jnp.where(high_lanes(value) == (side == 1), value, 0.0).astype(BF16)

    def both(product):
        return jnp.where(low, product[:vecs], product[vecs:])

    def pair_of(ref, node):
        return ref[node : node + 2].reshape(2 * rank, -1)

    loads[0].wait()
    points = [own[:, t * leaf_size : (t + 1) * leaf_size] for t in range(leaves)]
    before, centre, after = (pl.ds(i * leaves, leaves) for i in range(3))

    def to_neighbours(piece, rows):
        @pl.when(device + 1 < n_leaf)
        def _():
            send(
                piece, window.at[before, rows], side_send.at[0], side_recv.at[0], leaf_at(1), row
            )

        @pl.when(device > 0)
        def _():
            send(
                piece,
                window.at[after, rows],
                side_send.at[1],
                side_recv.at[1],
                leaf_at(n_leaf - 1),
                row,
            )

    def send_points(k):
        send(
            mine,
            window.at[centre, my_rows],
            gather_send,
            gather_recv.at[k - 1],
            device,
            lax.rem(row + k, n_rhs),
        )

    def tell_rows():
        for k in range(1, n_rhs):

            @pl.when(row >= k)
            def _(k=k):
                pl.semaphore_signal(
                    row_ready, inc=1, device_id=(device, row - k), device_id_type=MESH
                )

    def points_below():
        for t in range(leaves):
            mine[t] = points[t]
            window[leaves + t, my_rows] = points[t]
        for k in range(1, n_rhs):
            pl.when(row + k >= n_rhs)(functools.partial(send_points, k))
        to_neighbours(mine, my_rows)

    def points_above():
        @pl.when(row < n_rhs - 1)
        def _():
            pl.semaphore_wait(row_ready, n_rhs - 1 - row)
            for k in range(1, n_rhs):
                pl.when(row + k < n_rhs)(functools.partial(send_points, k))

    upper_half = level >= planes // 2
    early_planes = level < planes // 4

    @pl.when(early_planes)
    def _():
        pl.semaphore_wait(barrier, greetings)
        tell_rows()
        points_below()
        points_above()

    loads[1].wait()
    ups = []
    for c in range(leaves // 2):
        rows = jnp.concatenate([points[2 * c], points[2 * c + 1]], axis=0)
        ups.append(both(rows_by_rows(rows, pair_of(bases, 2 * c))))
    pairs = [pair.astype(BF16) for pair in ups]
    loads[2].wait()
    start = 0
    while len(pairs) > 1:
        nodes = len(pairs)
        pairs = [
            both(
                rows_by_rows(
                    jnp.concatenate([pairs[c], pairs[c + 1]], axis=0), pair_of(moves, start + c)
                )
            ).astype(BF16)
            for c in range(0, nodes, 2)
        ]
        start += nodes
    root = rows_by_rows(pairs[0], twice(moves[start]))

    loads[3].wait()
    plane_levels = plane.bit_length() - 1
    column_levels = planes.bit_length() - 1
    top_levels = plane_levels + column_levels

    def side_at(height):
        return lax.rem(lax.div(device, 1 << height - 1), 2)

    def lifted(value, height):
        return rows_by_rows(in_half(value, side_at(height)), twice(top_moves[height - 1]))

    def sibling_start(position, height):
        width = 1 << height - 1
        block = lax.div(position, width)
        return (block + 1 - 2 * lax.rem(block, 2)) * width

    shares = [root]
    for height in range(1, plane_levels + 1):
        shares.append(lifted(shares[-1], height))
    for height in range(1, plane_levels + 1):
        message_1[height - 1] = jnp.where(low, shares[height - 1], shares[plane_levels]).astype(BF16)
    arrived_1[place] = message_1[0]

    @pl.when(jnp.logical_not(early_planes))
    def _():
        pl.semaphore_wait(barrier, greetings)
        tell_rows()

    for height in range(plane_levels, 0, -1):
        for i in range(1 << height - 1):
            send(
                message_1.at[height - 1],
                arrived_1.at[place],
                send_1,
                recv_1,
                in_plane(sibling_start(place, height) + i),
                row,
            )

    def tell(other):
        pl.semaphore_signal(
            ready, inc=1, device_id=(in_column(other), row), device_id_type=MESH
        )

    loop(0, level, tell)
    for k in steps:

        @pl.when(device + k >= n_leaf)
        def _(k=k):
            pl.semaphore_signal(
                ready, inc=1, device_id=(leaf_at(k), row), device_id_type=MESH
            )

    for load in wants + loads[4:]:
        load.start()

    @pl.when(jnp.logical_not(early_planes))
    def _():
        points_below()

    for c, pair in enumerate(ups):
        turned = pltpu.roll(pair, rank, 1)
        for leaf, value in (
            (2 * c, jnp.where(low, pair, turned).astype(BF16)),
            (2 * c + 1, jnp.where(low, turned, pair).astype(BF16)),
        ):
            leaf_up[leaf] = value
            pool[leaf] = value

    def send_far(i):
        send(
            staged.at[i],
            pool.at[leaves + device],
            far_send,
            far_recv,
            leaf_at(offsets[i]),
            row,
        )

    def far_goes_early(i):
        offset = offsets[i]
        if offset <= 3:
            return None
        return device >= n_leaf - offset

    for i, offset in enumerate(offsets):
        wants[i].wait()
        staged[i] = leaf_up[want_s[i, device]]
        early = far_goes_early(i)
        if early is None:
            send_far(i)
        else:
            pl.when(early)(functools.partial(send_far, i))

    pl.when(jnp.logical_not(early_planes))(points_above)

    unit_rows = lax.broadcasted_iota(jnp.int32, (rank, 2 * rank), 0)
    unit_lanes = lax.broadcasted_iota(jnp.int32, (rank, 2 * rank), 1)
    unit = jnp.where((unit_lanes == unit_rows) | (unit_lanes == unit_rows + rank), 1.0, 0.0)
    lifts = [unit]
    for height in range(plane_levels + 1, top_levels):
        lifts.append(lifted(lifts[-1], height))
    lift = twice(jnp.concatenate([each.astype(BF16) for each in lifts], axis=1))
    wait_bytes(arrived_1.at[pl.ds(0, plane - 1)], recv_1)
    plane_up = in_half(sum(arrived_1[i].astype(F32) for i in range(plane)), 1)
    above_plane = rows_by_cols(plane_up, lift).astype(BF16)
    for i in range(column_levels):
        message_2[i] = above_plane[:, i * 2 * rank : (i + 1) * 2 * rank]

    def send_column(height):
        first = sibling_start(level, height)

        def one(i):
            send(
                message_2.at[height - 1],
                arrived_2.at[level],
                send_2,
                recv_2,
                in_column(first + i),
                row,
            )

        width = 1 << height - 1

        def in_turn(i):
            aside = lax.div(i + 1, 2) * (2 * lax.rem(i, 2) - 1)
            one(lax.rem(lax.rem(level, width) + aside + width, width))

        loop(0, width, in_turn)

    for height in range(column_levels, 0, -1):
        pl.when(side_at(plane_levels + height) == 1)(functools.partial(send_column, height))

    for k in (1, 3, 2):
        if k < n_rhs:
            theirs = pl.ds(pl.multiple_of(lax.rem(row + n_rhs - k, n_rhs) * vecs, vecs), vecs)
            piece = window.at[centre, theirs]
            wait_bytes(piece, gather_recv.at[k - 1])
            to_neighbours(piece, theirs)

    loads[8].wait()

    def term(sibling, height):
        return rows_by_rows(
            in_half(sibling, side_at(height)), twice(top_couplings[height - 1])
        )

    def split(pair):
        high = high_lanes(pair)
        return jnp.concatenate(
            [jnp.where(high, 0.0, pair), jnp.where(high, pair, 0.0)], axis=0
        ).astype(BF16)

    down = in_half(term(unit, top_levels), side_at(top_levels))
    for height in range(top_levels - 1, 0, -1):
        spread = rows_by_cols(down, twice(top_moves[height - 1]))
        if height > plane_levels:
            spread = jnp.concatenate([term(unit, height), spread], axis=0)
        else:
            first = sibling_start(place, height)
            sibling = sum(arrived_1[first + i].astype(F32) for i in range(1 << height - 1))
            sibling = rows_by_cols(in_half(sibling, 0), twice(unit.astype(BF16)))
            own_term = term(sibling, height)
            if height == plane_levels:
                spread = jnp.concatenate([own_term, spread], axis=0)
            else:
                spread = jnp.concatenate([spread[:vecs] + own_term, spread[vecs:]], axis=0)
        down = in_half(spread, side_at(height))
    pairs = [rows_by_cols(down, twice(moves[start]))]
    rows_now = pairs[0].shape[0]
    while len(pairs) < leaves // 2:
        start -= 2 * len(pairs)
        spreads = [
            rows_by_cols(split(pair), pair_of(moves, start + 2 * c))
            for c, pair in enumerate(pairs)
        ]
        pairs = [half for both_now in spreads for half in (both_now[:rows_now], both_now[rows_now:])]
    for c, pair in enumerate(pairs):
        coupled[c] = pair[:vecs]
        wide[c] = pair[vecs:].astype(BF16)

    above = planes - 1 - level + len(steps) - behind

    def send_above():
        @pl.when(above > 0)
        def _():
            pl.semaphore_wait(ready, above)

        for height in range(column_levels, 0, -1):
            pl.when(side_at(plane_levels + height) == 0)(functools.partial(send_column, height))
        for i in range(len(offsets)):
            early = far_goes_early(i)
            if early is not None:
                pl.when(jnp.logical_not(early))(functools.partial(send_far, i))

    pl.when(jnp.logical_not(early_planes))(send_above)

    loads[5].wait()
    loads[6].wait()

    @pl.when(device > 0)
    def _():
        wait_bytes(window.at[before], side_recv.at[0])

    @pl.when(device + 1 < n_leaf)
    def _():
        wait_bytes(window.at[after], side_recv.at[1])

    slots = blocks.shape[0]
    first_leaf = (device - 1) * leaves
    width = NEAR_CHUNK * leaf_size
    for chunk in range(leaves // NEAR_CHUNK):
        for leaf in range(chunk * NEAR_CHUNK, (chunk + 1) * NEAR_CHUNK):
            sources = jnp.concatenate(
                [
                    window[(src_s[q, leaf] - first_leaf) & (window.shape[0] - 1)]
                    for q in range(slots)
                ],
                axis=1,
            )
            matrix = jnp.concatenate([blocks[q, leaf] for q in range(slots)], axis=1)
            partial[:, leaf * leaf_size : (leaf + 1) * leaf_size] = rows_by_rows(
                sources, matrix
            ).astype(BF16)
        cols = pl.ds(chunk * width, width)
        for k in (2, 1, 3):
            if k < n_rhs:
                target = lax.rem(row + k, n_rhs)
                theirs = pl.ds(pl.multiple_of(target * vecs, vecs), vecs)
                send(
                    partial.at[theirs, cols],
                    others.at[k - 1, :, cols],
                    part_send,
                    part_recv,
                    device,
                    target,
                )

    pl.when(early_planes)(send_above)

    loads[4].wait()
    loads[7].wait()
    wait_bytes(staged, far_recv)
    far = couplings.shape[2] // rank

    def far_block(leaf, f):
        return pool[far_s[f, leaf]].astype(F32)

    def far_row(leaf):
        return jnp.concatenate(
            [
                jnp.where(low, far_block(leaf, f), far_block(leaf, f + 1)).astype(BF16)
                for f in range(0, far, 2)
            ],
            axis=1,
        )

    for c in range(leaves // 2):
        sources = jnp.concatenate([far_row(2 * c), far_row(2 * c + 1)], axis=0)
        coupled[c] = coupled[c] + both(rows_by_rows(sources, pair_of(couplings, 2 * c)))

    def add_near():
        wait_bytes(others, part_recv)
        for leaf in range(leaves):
            cols = slice(leaf * leaf_size, (leaf + 1) * leaf_size)
            total = out[:, cols] + partial[my_rows, cols].astype(F32)
            for k in range(n_rhs - 1):
                total = total + others[k, :, cols].astype(F32)
            out[:, cols] = total

    out[...] = jnp.zeros_like(out)
    pl.when(jnp.logical_not(upper_half))(add_near)

    wait_bytes(arrived_2.at[pl.ds(0, planes - 1)], recv_2)
    siblings = []
    for height in range(1, column_levels + 1):
        first = sibling_start(level, height)
        siblings.append(sum(arrived_2[first + i].astype(F32) for i in range(1 << height - 1)))
    siblings = jnp.concatenate(
        [jnp.where(low, *siblings[i : i + 2]) for i in range(0, column_levels, 2)], axis=1
    ).astype(BF16)
    for c in range(leaves // 2):
        pair = coupled[c] + rows_by_cols(siblings, wide[c])
        far_part = rows_by_cols(split(pair), pair_of(bases, 2 * c))
        for leaf, value in ((2 * c, far_part[:vecs]), (2 * c + 1, far_part[vecs:])):
            cols = slice(leaf * leaf_size, (leaf + 1) * leaf_size)
            out[:, cols] = out[:, cols] + value

    pl.when(upper_half)(add_near)

    if n_rhs > 1:
        wait_bytes(others, gather_send)
        wait_bytes(others, part_send)

    @pl.when(device + 1 < n_leaf)
    def _():
        wait_bytes(window.at[before], side_send.at[0])

    @pl.when(device > 0)
    def _():
        wait_bytes(window.at[after], side_send.at[1])

    wait_bytes(staged, far_send)
    wait_bytes(arrived_1.at[pl.ds(0, plane - 1)], send_1)
    wait_bytes(arrived_2.at[pl.ds(0, planes - 1)], send_2)


def local(n_leaf, n_rhs, plane, *arrays):
    (vectors, near_blocks, near_src, basis, local_transfer, leaf_coupling, far_slot) = arrays[:7]
    want_leaf, top_transfer, top_coupling = arrays[7:]
    vecs, span = vectors.shape
    leaves, rank, leaf_size = basis.shape
    far_slot = far_slot.T
    planes = n_leaf // plane
    levels = plane.bit_length() - 1, planes.bit_length() - 1
    dma = pltpu.SemaphoreType.DMA
    scratch = [
        pltpu.VMEM((vecs, span), BF16),
        pltpu.VMEM((leaves, vecs, leaf_size), BF16),
        pltpu.VMEM((4 * leaves, n_rhs * vecs, leaf_size), BF16),
        pltpu.VMEM(near_blocks.shape, BF16),
        pltpu.VMEM(basis.shape, BF16),
        pltpu.VMEM(local_transfer.shape, BF16),
        pltpu.VMEM(leaf_coupling.shape, BF16),
        pltpu.VMEM(top_transfer.shape[1:], BF16),
        pltpu.VMEM(top_coupling.shape[1:], BF16),
        pltpu.SMEM(near_src.shape, jnp.int32),
        pltpu.SMEM(far_slot.shape, jnp.int32),
        pltpu.SMEM((7, n_leaf), jnp.int32),
        pltpu.VMEM((leaves, vecs, 2 * rank), BF16),
        pltpu.VMEM((leaves + n_leaf, vecs, 2 * rank), BF16),
        pltpu.VMEM((7, vecs, 2 * rank), BF16),
        pltpu.VMEM((levels[0], vecs, 2 * rank), BF16),
        pltpu.VMEM((plane, vecs, 2 * rank), BF16),
        pltpu.VMEM((levels[1], vecs, 2 * rank), BF16),
        pltpu.VMEM((planes, vecs, 2 * rank), BF16),
        pltpu.VMEM((leaves // 2, vecs, 2 * rank), F32),
        pltpu.VMEM((leaves // 2, levels[1] * rank, 2 * rank), BF16),
        pltpu.VMEM((n_rhs * vecs, span), BF16),
        pltpu.VMEM((max(n_rhs - 1, 1), vecs, span), BF16),
        dma((9,)),
        dma((7,)),
        dma,
        dma((max(n_rhs - 1, 1),)),
        dma((2,)),
        dma((2,)),
        dma,
        dma,
        dma,
        dma,
        dma,
        dma,
        dma,
        dma,
        pltpu.SemaphoreType.REGULAR,
        pltpu.SemaphoreType.REGULAR,
    ]
    return pl.pallas_call(
        functools.partial(kernel, n_leaf, n_rhs, plane),
        out_shape=pltpu.VMEM((vecs, span), F32),
        in_specs=[pl.BlockSpec(memory_space=pltpu.HBM)] * 10,
        out_specs=pl.BlockSpec(memory_space=pltpu.VMEM),
        scratch_shapes=scratch,
        compiler_params=pltpu.CompilerParams(
            collective_id=0, has_side_effects=True, vmem_limit_bytes=60 << 20
        ),
        name="hierarchical_product",
    )(
        vectors,
        near_blocks,
        near_src,
        basis,
        local_transfer,
        leaf_coupling,
        far_slot,
        want_leaf,
        top_transfer,
        top_coupling,
    )


def solution(mesh):
    in_specs = (
        P("rhs", "leaf"),
        P("rhs", "leaf", None, None),
        P("rhs", "leaf"),
        P("leaf", None, None),
        P("leaf", None, None),
        P("leaf", None, None),
        P("leaf", None),
        P(),
        P("leaf", None, None, None),
        P("leaf", None, None, None),
    )
    body = functools.partial(local, mesh.shape["leaf"], mesh.shape["rhs"], 8)
    return jax.shard_map(
        body, mesh=mesh, in_specs=in_specs, out_specs=P("rhs", "leaf"), check_vma=False
    )
```

```python
import functools

import jax
import jax.numpy as jnp
from jax import lax
from jax.experimental import pallas as pl
from jax.experimental.pallas import tpu as pltpu
from jax.sharding import PartitionSpec as P

MESH = pl.DeviceIdType.MESH
F32 = jnp.float32
BF16 = jnp.bfloat16
NEAR_CHUNK = 8


def rows_by_rows(lhs, rhs):
    return lax.dot_general(lhs, rhs, (((1,), (1,)), ((), ())), preferred_element_type=F32)


def rows_by_cols(lhs, rhs):
    return lax.dot_general(lhs, rhs, (((1,), (0,)), ((), ())), preferred_element_type=F32)


def twice(matrix):
    return jnp.concatenate([matrix, matrix], axis=0)


def kernel(
    n_leaf,
    n_rhs,
    plane,
    vectors,
    near_blocks,
    near_src,
    basis,
    local_transfer,
    leaf_coupling,
    far_slot,
    want_leaf,
    top_transfer,
    top_coupling,
    out,
    own,
    mine,
    window,
    blocks,
    bases,
    moves,
    couplings,
    top_moves,
    top_couplings,
    src_s,
    far_s,
    want_s,
    leaf_up,
    pool,
    staged,
    message_1,
    arrived_1,
    message_2,
    arrived_2,
    coupled,
    wide,
    partial,
    others,
    load_sem,
    want_sem,
    gather_send,
    gather_recv,
    side_send,
    side_recv,
    far_send,
    far_recv,
    send_1,
    recv_1,
    send_2,
    recv_2,
    part_send,
    part_recv,
    ready,
    row_ready,
):
    vecs, span = vectors.shape
    leaves, rank, leaf_size = basis.shape
    device = lax.axis_index("leaf")
    row = lax.axis_index("rhs")
    planes = n_leaf // plane
    place = lax.rem(device, plane)
    level = lax.div(device, plane)
    offsets = [1, 2, 3, n_leaf - 1, n_leaf - 2, n_leaf - 3, n_leaf // 2]
    my_rows = pl.ds(pl.multiple_of(row * vecs, vecs), vecs)

    def leaf_at(offset):
        return lax.rem(device + offset, n_leaf)

    def in_plane(where):
        return level * plane + where

    def in_column(where):
        return where * plane + place

    loads = [
        pltpu.make_async_copy(vectors, own, load_sem.at[0]),
        pltpu.make_async_copy(basis, bases, load_sem.at[1]),
        pltpu.make_async_copy(local_transfer, moves, load_sem.at[2]),
        pltpu.make_async_copy(top_transfer.at[0], top_moves, load_sem.at[3]),
        pltpu.make_async_copy(far_slot, far_s, load_sem.at[4]),
        pltpu.make_async_copy(near_src, src_s, load_sem.at[5]),
        pltpu.make_async_copy(near_blocks, blocks, load_sem.at[6]),
        pltpu.make_async_copy(leaf_coupling, couplings, load_sem.at[7]),
        pltpu.make_async_copy(top_coupling.at[0], top_couplings, load_sem.at[8]),
    ]
    wants = [
        pltpu.make_async_copy(
            want_leaf.at[pl.ds(leaf_at(offset), 1)], want_s.at[pl.ds(i, 1)], want_sem.at[i]
        )
        for i, offset in enumerate(offsets)
    ]
    for load in loads[:4]:
        load.start()

    barrier = pltpu.get_barrier_semaphore()

    def greet(leaf_index, rhs_index):
        pl.semaphore_signal(
            barrier, inc=1, device_id=(leaf_index, rhs_index), device_id_type=MESH
        )

    def loop(first, last, step):
        def body(i, carry):
            step(i)
            return carry

        lax.fori_loop(first, last, body, 0)

    steps = range(1, 4)
    for k in range(1, plane):
        greet(in_plane(lax.rem(place + k, plane)), row)
    for k in range(1, n_rhs):
        pl.when(row + k < n_rhs)(functools.partial(greet, device, row + k))
    for k in steps:
        greet(leaf_at(n_leaf - k), row)
        pl.when(device + k < n_leaf)(functools.partial(greet, leaf_at(k), row))
    loop(level + 1, planes, lambda other: greet(in_column(other), row))
    behind = sum((device >= k).astype(jnp.int32) for k in steps)
    greetings = row + (plane - 1) + len(steps) + behind + level

    def send(src, dst, send_sem, recv_sem, leaf_index, rhs_index):
        pltpu.make_async_remote_copy(
            src_ref=src,
            dst_ref=dst,
            send_sem=send_sem,
            recv_sem=recv_sem,
            device_id=(leaf_index, rhs_index),
            device_id_type=MESH,
        ).start()

    def wait_bytes(ref, sem):
        pltpu.make_async_copy(ref, ref, sem).wait()

    lanes = lax.broadcasted_iota(jnp.int32, (vecs, 2 * rank), 1)
    low = lanes < rank

    def high_lanes(value):
        return lax.broadcasted_iota(jnp.int32, value.shape, 1) >= rank

    def in_half(value, side):
        return jnp.where(high_lanes(value) == (side == 1), value, 0.0).astype(BF16)

    def both(product):
        return jnp.where(low, product[:vecs], product[vecs:])

    def pair_of(ref, node):
        return ref[node : node + 2].reshape(2 * rank, -1)

    loads[0].wait()
    points = [own[:, t * leaf_size : (t + 1) * leaf_size] for t in range(leaves)]
    before, centre, after = (pl.ds(i * leaves, leaves) for i in range(3))

    def to_neighbours(piece, rows):
        @pl.when(device + 1 < n_leaf)
        def _():
            send(
                piece, window.at[before, rows], side_send.at[0], side_recv.at[0], leaf_at(1), row
            )

        @pl.when(device > 0)
        def _():
            send(
                piece,
                window.at[after, rows],
                side_send.at[1],
                side_recv.at[1],
                leaf_at(n_leaf - 1),
                row,
            )

    def send_points(k):
        send(
            mine,
            window.at[centre, my_rows],
            gather_send,
            gather_recv.at[k - 1],
            device,
            lax.rem(row + k, n_rhs),
        )

    def tell_rows():
        for k in range(1, n_rhs):

            @pl.when(row >= k)
            def _(k=k):
                pl.semaphore_signal(
                    row_ready, inc=1, device_id=(device, row - k), device_id_type=MESH
                )

    def points_below():
        for t in range(leaves):
            mine[t] = points[t]
            window[leaves + t, my_rows] = points[t]
        for k in range(1, n_rhs):
            pl.when(row + k >= n_rhs)(functools.partial(send_points, k))
        to_neighbours(mine, my_rows)

    def points_above():
        @pl.when(row < n_rhs - 1)
        def _():
            pl.semaphore_wait(row_ready, n_rhs - 1 - row)
            for k in range(1, n_rhs):
                pl.when(row + k < n_rhs)(functools.partial(send_points, k))

    upper_half = level >= planes // 2
    early_planes = level < planes // 4

    @pl.when(early_planes)
    def _():
        pl.semaphore_wait(barrier, greetings)
        tell_rows()
        points_below()
        points_above()

    loads[1].wait()
    ups = []
    for c in range(leaves // 2):
        rows = jnp.concatenate([points[2 * c], points[2 * c + 1]], axis=0)
        ups.append(both(rows_by_rows(rows, pair_of(bases, 2 * c))))
    pairs = [pair.astype(BF16) for pair in ups]
    loads[2].wait()
    start = 0
    while len(pairs) > 1:
        nodes = len(pairs)
        pairs = [
            both(
                rows_by_rows(
                    jnp.concatenate([pairs[c], pairs[c + 1]], axis=0), pair_of(moves, start + c)
                )
            ).astype(BF16)
            for c in range(0, nodes, 2)
        ]
        start += nodes
    root = rows_by_rows(pairs[0], twice(moves[start]))

    loads[3].wait()
    plane_levels = plane.bit_length() - 1
    column_levels = planes.bit_length() - 1
    top_levels = plane_levels + column_levels

    def side_at(height):
        return lax.rem(lax.div(device, 1 << height - 1), 2)

    def lifted(value, height):
        return rows_by_rows(in_half(value, side_at(height)), twice(top_moves[height - 1]))

    def sibling_start(position, height):
        width = 1 << height - 1
        block = lax.div(position, width)
        return (block + 1 - 2 * lax.rem(block, 2)) * width

    shares = [root]
    for height in range(1, plane_levels + 1):
        shares.append(lifted(shares[-1], height))
    for height in range(1, plane_levels + 1):
        message_1[height - 1] = jnp.where(low, shares[height - 1], shares[plane_levels]).astype(BF16)
    arrived_1[place] = message_1[0]

    @pl.when(jnp.logical_not(early_planes))
    def _():
        pl.semaphore_wait(barrier, greetings)
        tell_rows()

    for height in range(plane_levels, 0, -1):
        for i in range(1 << height - 1):
            send(
                message_1.at[height - 1],
                arrived_1.at[place],
                send_1,
                recv_1,
                in_plane(sibling_start(place, height) + i),
                row,
            )

    def tell(other):
        pl.semaphore_signal(
            ready, inc=1, device_id=(in_column(other), row), device_id_type=MESH
        )

    loop(0, level, tell)
    for k in steps:

        @pl.when(device + k >= n_leaf)
        def _(k=k):
            pl.semaphore_signal(
                ready, inc=1, device_id=(leaf_at(k), row), device_id_type=MESH
            )

    for load in wants + loads[4:]:
        load.start()

    @pl.when(jnp.logical_not(early_planes))
    def _():
        points_below()

    for c, pair in enumerate(ups):
        turned = pltpu.roll(pair, rank, 1)
        for leaf, value in (
            (2 * c, jnp.where(low, pair, turned).astype(BF16)),
            (2 * c + 1, jnp.where(low, turned, pair).astype(BF16)),
        ):
            leaf_up[leaf] = value
            pool[leaf] = value

    def send_far(i):
        send(
            staged.at[i],
            pool.at[leaves + device],
            far_send,
            far_recv,
            leaf_at(offsets[i]),
            row,
        )

    def far_goes_early(i):
        offset = offsets[i]
        if offset <= 3:
            return None
        return device >= n_leaf - offset

    for i, offset in enumerate(offsets):
        wants[i].wait()
        staged[i] = leaf_up[want_s[i, device]]
        early = far_goes_early(i)
        if early is None:
            send_far(i)
        else:
            pl.when(early)(functools.partial(send_far, i))

    pl.when(jnp.logical_not(early_planes))(points_above)

    unit_rows = lax.broadcasted_iota(jnp.int32, (rank, 2 * rank), 0)
    unit_lanes = lax.broadcasted_iota(jnp.int32, (rank, 2 * rank), 1)
    unit = jnp.where((unit_lanes == unit_rows) | (unit_lanes == unit_rows + rank), 1.0, 0.0)
    lifts = [unit]
    for height in range(plane_levels + 1, top_levels):
        lifts.append(lifted(lifts[-1], height))
    lift = twice(jnp.concatenate([each.astype(BF16) for each in lifts], axis=1))
    wait_bytes(arrived_1.at[pl.ds(0, plane - 1)], recv_1)
    plane_up = in_half(sum(arrived_1[i].astype(F32) for i in range(plane)), 1)
    above_plane = rows_by_cols(plane_up, lift).astype(BF16)
    for i in range(column_levels):
        message_2[i] = above_plane[:, i * 2 * rank : (i + 1) * 2 * rank]

    def send_column(height):
        first = sibling_start(level, height)

        def one(i):
            send(
                message_2.at[height - 1],
                arrived_2.at[level],
                send_2,
                recv_2,
                in_column(first + i),
                row,
            )

        width = 1 << height - 1

        def in_turn(i):
            aside = lax.div(i + 1, 2) * (2 * lax.rem(i, 2) - 1)
            one(lax.rem(lax.rem(level, width) + aside + width, width))

        loop(0, width, in_turn)

    for height in range(column_levels, 0, -1):
        pl.when(side_at(plane_levels + height) == 1)(functools.partial(send_column, height))

    for k in (1, 3, 2):
        if k < n_rhs:
            theirs = pl.ds(pl.multiple_of(lax.rem(row + n_rhs - k, n_rhs) * vecs, vecs), vecs)
            piece = window.at[centre, theirs]
            wait_bytes(piece, gather_recv.at[k - 1])
            to_neighbours(piece, theirs)

    loads[8].wait()

    def term(sibling, height):
        return rows_by_rows(
            in_half(sibling, side_at(height)), twice(top_couplings[height - 1])
        )

    def split(pair):
        high = high_lanes(pair)
        return jnp.concatenate(
            [jnp.where(high, 0.0, pair), jnp.where(high, pair, 0.0)], axis=0
        ).astype(BF16)

    down = in_half(term(unit, top_levels), side_at(top_levels))
    for height in range(top_levels - 1, 0, -1):
        spread = rows_by_cols(down, twice(top_moves[height - 1]))
        if height > plane_levels:
            spread = jnp.concatenate([term(unit, height), spread], axis=0)
        else:
            first = sibling_start(place, height)
            sibling = sum(arrived_1[first + i].astype(F32) for i in range(1 << height - 1))
            sibling = rows_by_cols(in_half(sibling, 0), twice(unit.astype(BF16)))
            own_term = term(sibling, height)
            if height == plane_levels:
                spread = jnp.concatenate([own_term, spread], axis=0)
            else:
                spread = jnp.concatenate([spread[:vecs] + own_term, spread[vecs:]], axis=0)
        down = in_half(spread, side_at(height))
    pairs = [rows_by_cols(down, twice(moves[start]))]
    rows_now = pairs[0].shape[0]
    while len(pairs) < leaves // 2:
        start -= 2 * len(pairs)
        spreads = [
            rows_by_cols(split(pair), pair_of(moves, start + 2 * c))
            for c, pair in enumerate(pairs)
        ]
        pairs = [half for both_now in spreads for half in (both_now[:rows_now], both_now[rows_now:])]
    for c, pair in enumerate(pairs):
        coupled[c] = pair[:vecs]
        wide[c] = pair[vecs:].astype(BF16)

    above = planes - 1 - level + len(steps) - behind

    def send_above():
        @pl.when(above > 0)
        def _():
            pl.semaphore_wait(ready, above)

        for height in range(column_levels, 0, -1):
            pl.when(side_at(plane_levels + height) == 0)(functools.partial(send_column, height))
        for i in range(len(offsets)):
            early = far_goes_early(i)
            if early is not None:
                pl.when(jnp.logical_not(early))(functools.partial(send_far, i))

    pl.when(jnp.logical_not(early_planes))(send_above)

    loads[5].wait()
    loads[6].wait()

    @pl.when(device > 0)
    def _():
        wait_bytes(window.at[before], side_recv.at[0])

    @pl.when(device + 1 < n_leaf)
    def _():
        wait_bytes(window.at[after], side_recv.at[1])

    slots = blocks.shape[0]
    first_leaf = (device - 1) * leaves
    width = NEAR_CHUNK * leaf_size
    for chunk in range(leaves // NEAR_CHUNK):
        for leaf in range(chunk * NEAR_CHUNK, (chunk + 1) * NEAR_CHUNK):
            sources = jnp.concatenate(
                [
                    window[(src_s[q, leaf] - first_leaf) & (window.shape[0] - 1)]
                    for q in range(slots)
                ],
                axis=1,
            )
            matrix = jnp.concatenate([blocks[q, leaf] for q in range(slots)], axis=1)
            partial[:, leaf * leaf_size : (leaf + 1) * leaf_size] = rows_by_rows(
                sources, matrix
            ).astype(BF16)
        cols = pl.ds(chunk * width, width)
        for k in (2, 1, 3):
            if k < n_rhs:
                target = lax.rem(row + k, n_rhs)
                theirs = pl.ds(pl.multiple_of(target * vecs, vecs), vecs)
                send(
                    partial.at[theirs, cols],
                    others.at[k - 1, :, cols],
                    part_send,
                    part_recv,
                    device,
                    target,
                )

    pl.when(early_planes)(send_above)

    loads[4].wait()
    loads[7].wait()
    wait_bytes(staged, far_recv)
    far = couplings.shape[2] // rank

    def far_block(leaf, f):
        return pool[far_s[f, leaf]].astype(F32)

    def far_row(leaf):
        return jnp.concatenate(
            [
                jnp.where(low, far_block(leaf, f), far_block(leaf, f + 1)).astype(BF16)
                for f in range(0, far, 2)
            ],
            axis=1,
        )

    for c in range(leaves // 2):
        sources = jnp.concatenate([far_row(2 * c), far_row(2 * c + 1)], axis=0)
        coupled[c] = coupled[c] + both(rows_by_rows(sources, pair_of(couplings, 2 * c)))

    def add_near():
        wait_bytes(others, part_recv)
        for leaf in range(leaves):
            cols = slice(leaf * leaf_size, (leaf + 1) * leaf_size)
            total = out[:, cols] + partial[my_rows, cols].astype(F32)
            for k in range(n_rhs - 1):
                total = total + others[k, :, cols].astype(F32)
            out[:, cols] = total

    out[...] = jnp.zeros_like(out)
    pl.when(jnp.logical_not(upper_half))(add_near)

    wait_bytes(arrived_2.at[pl.ds(0, planes - 1)], recv_2)
    siblings = []
    for height in range(1, column_levels + 1):
        first = sibling_start(level, height)
        siblings.append(sum(arrived_2[first + i].astype(F32) for i in range(1 << height - 1)))
    siblings = jnp.concatenate(
        [jnp.where(low, *siblings[i : i + 2]) for i in range(0, column_levels, 2)], axis=1
    ).astype(BF16)
    for c in range(leaves // 2):
        pair = coupled[c] + rows_by_cols(siblings, wide[c])
        far_part = rows_by_cols(split(pair), pair_of(bases, 2 * c))
        for leaf, value in ((2 * c, far_part[:vecs]), (2 * c + 1, far_part[vecs:])):
            cols = slice(leaf * leaf_size, (leaf + 1) * leaf_size)
            out[:, cols] = out[:, cols] + value

    pl.when(upper_half)(add_near)

    if n_rhs > 1:
        wait_bytes(others, gather_send)
        wait_bytes(others, part_send)

    @pl.when(device + 1 < n_leaf)
    def _():
        wait_bytes(window.at[before], side_send.at[0])

    @pl.when(device > 0)
    def _():
        wait_bytes(window.at[after], side_send.at[1])

    wait_bytes(staged, far_send)
    wait_bytes(arrived_1.at[pl.ds(0, plane - 1)], send_1)
    wait_bytes(arrived_2.at[pl.ds(0, planes - 1)], send_2)


def local(n_leaf, n_rhs, plane, *arrays):
    (vectors, near_blocks, near_src, basis, local_transfer, leaf_coupling, far_slot) = arrays[:7]
    want_leaf, top_transfer, top_coupling = arrays[7:]
    vecs, span = vectors.shape
    leaves, rank, leaf_size = basis.shape
    far_slot = far_slot.T
    planes = n_leaf // plane
    levels = plane.bit_length() - 1, planes.bit_length() - 1
    dma = pltpu.SemaphoreType.DMA
    scratch = [
        pltpu.VMEM((vecs, span), BF16),
        pltpu.VMEM((leaves, vecs, leaf_size), BF16),
        pltpu.VMEM((4 * leaves, n_rhs * vecs, leaf_size), BF16),
        pltpu.VMEM(near_blocks.shape, BF16),
        pltpu.VMEM(basis.shape, BF16),
        pltpu.VMEM(local_transfer.shape, BF16),
        pltpu.VMEM(leaf_coupling.shape, BF16),
        pltpu.VMEM(top_transfer.shape[1:], BF16),
        pltpu.VMEM(top_coupling.shape[1:], BF16),
        pltpu.SMEM(near_src.shape, jnp.int32),
        pltpu.SMEM(far_slot.shape, jnp.int32),
        pltpu.SMEM((7, n_leaf), jnp.int32),
        pltpu.VMEM((leaves, vecs, 2 * rank), BF16),
        pltpu.VMEM((leaves + n_leaf, vecs, 2 * rank), BF16),
        pltpu.VMEM((7, vecs, 2 * rank), BF16),
        pltpu.VMEM((levels[0], vecs, 2 * rank), BF16),
        pltpu.VMEM((plane, vecs, 2 * rank), BF16),
        pltpu.VMEM((levels[1], vecs, 2 * rank), BF16),
        pltpu.VMEM((planes, vecs, 2 * rank), BF16),
        pltpu.VMEM((leaves // 2, vecs, 2 * rank), F32),
        pltpu.VMEM((leaves // 2, levels[1] * rank, 2 * rank), BF16),
        pltpu.VMEM((n_rhs * vecs, span), BF16),
        pltpu.VMEM((max(n_rhs - 1, 1), vecs, span), BF16),
        dma((9,)),
        dma((7,)),
        dma,
        dma((max(n_rhs - 1, 1),)),
        dma((2,)),
        dma((2,)),
        dma,
        dma,
        dma,
        dma,
        dma,
        dma,
        dma,
        dma,
        pltpu.SemaphoreType.REGULAR,
        pltpu.SemaphoreType.REGULAR,
    ]
    return pl.pallas_call(
        functools.partial(kernel, n_leaf, n_rhs, plane),
        out_shape=pltpu.VMEM((vecs, span), F32),
        in_specs=[pl.BlockSpec(memory_space=pltpu.HBM)] * 10,
        out_specs=pl.BlockSpec(memory_space=pltpu.VMEM),
        scratch_shapes=scratch,
        compiler_params=pltpu.CompilerParams(
            collective_id=0, has_side_effects=True, vmem_limit_bytes=60 << 20
        ),
        name="hierarchical_product",
    )(
        vectors,
        near_blocks,
        near_src,
        basis,
        local_transfer,
        leaf_coupling,
        far_slot,
        want_leaf,
        top_transfer,
        top_coupling,
    )


def solution(mesh):
    in_specs = (
        P("rhs", "leaf"),
        P("rhs", "leaf", None, None),
        P("rhs", "leaf"),
        P("leaf", None, None),
        P("leaf", None, None),
        P("leaf", None, None),
        P("leaf", None),
        P(),
        P("leaf", None, None, None),
        P("leaf", None, None, None),
    )
    body = functools.partial(local, mesh.shape["leaf"], mesh.shape["rhs"], 8)
    return jax.shard_map(
        body, mesh=mesh, in_specs=in_specs, out_specs=P("rhs", "leaf"), check_vma=False
    )
```
